256 devices in a mesh: ctx: 64 (over x, y_lo, z), ch: 4 (over y_hi, core).
Axes of the slice: x: 4, y: 4 (y_hi: 2, y_lo: 2; y = y_hi * 2 + y_lo), z: 8, core: 2. Of those that a mesh axis runs over, the one named last changes fastest.
Arguments:
- token_ids: int32 [8192], P('ctx'), may hold values from 0 to 511
- tables: bfloat16 [512, 3, 8192], P(None, None, 'ch'), may hold values from -6 to 6
- filter_long: bfloat16 [8192, 8192], P('ctx', 'ch'), may hold values from -0.0625 to 0.0625
- skip_long: float32 [8192], P('ch'), may hold values from -4 to 4
- taps_in: float32 [3, 3, 8192], P(None, None, 'ch'), may hold values from -3 to 3
- projection: bfloat16 [8192, 3, 1024], P('ch', None, 'ctx'), may hold values from -0.0625 to 0.0625
- taps_proj: float32 [3, 3, 1024], P(None, None, 'ch'), may hold values from -3 to 3
- taps_short: float32 [7, 1024], P(None, 'ch'), may hold values from -2 to 2
- skip_short: float32 [1024], P('ch'), may hold values from -4 to 4
Outputs:
- mixed_out: bfloat16 [8192, 1024], P('ctx', 'ch')
The draws below stay inside these ranges and needn't reach their ends.
All inputs are finite; a program needn't handle non-finite values.
Results may differ from the reference program's by a relative error of at most 0.025.
Values may be sent and summed in bfloat16 or wider, within the bound.
A program may use at most 128 MiB of HBM per device.

```python
import jax
import jax.numpy as jnp
from jax import lax

VOCAB = 512
WIDTH = 8192
SLAB = 1024
FEAT = 3
SHORT = 7
SEQ = 8192


def with_ends(entries, key, smallest, high):
    shape = entries.shape
    place = [jax.random.randint(jax.random.fold_in(key, axis), (), 0, shape[axis]) for axis in range(len(shape))]
    entries = entries.at[tuple(place)].set(smallest)
    longest = shape.index(max(shape))
    place[longest] = (place[longest] + 1) % shape[longest]
    return entries.at[tuple(place)].set(high)


def steps_of(rng, shape, cuts, low, top_value):
    loudness, own = 1.0, jax.random.fold_in(rng, 6)
    for position, shards_of in cuts:
        steps = jnp.exp(jax.random.uniform(jax.random.fold_in(own, position), (shards_of,), jnp.float32, low / len(cuts), top_value / len(cuts)))
        loudness = loudness * jnp.repeat(steps, shape[position] // shards_of).reshape([-1 if axis == position else 1 for axis in range(len(shape))])
    return loudness


def bell_draw(stream_key, extent, width, limit, pieces=(), held_as=jnp.bfloat16):
    drawn = width * jax.random.normal(stream_key, extent, jnp.float32)
    if pieces:
        drawn = drawn * steps_of(stream_key, extent, pieces, -0.22, 0.18)
    return jnp.clip(drawn, -limit, limit).astype(held_as)


def setup_inputs(seed: int = 0) -> dict:
    seeds = jax.random.split(jax.random.key(seed), 10)
    token_ids = with_ends(jax.random.randint(seeds[0], (SEQ,), 0, VOCAB), jax.random.fold_in(seeds[0], 1), 0, VOCAB - 1).astype(jnp.int32)
    tables = bell_draw(seeds[1], (VOCAB, 3, WIDTH), 1.0, 6.0, ((2, 4),))
    filter_long = bell_draw(seeds[2], (SEQ, WIDTH), SEQ ** -0.5, 0.0625, ((0, 64), (1, 4)))
    skip_long = bell_draw(seeds[3], (WIDTH,), 1.0, 4.0, ((0, 4),), jnp.float32)
    taps_in = bell_draw(seeds[4], (FEAT, 3, WIDTH), 0.6, 3.0, ((2, 4),), jnp.float32)
    projection = bell_draw(seeds[5], (WIDTH, 3, SLAB), WIDTH ** -0.5, 0.0625, ((0, 4), (2, 64)))
    taps_proj = bell_draw(seeds[6], (FEAT, 3, SLAB), 0.6, 3.0, ((2, 4),), jnp.float32)
    taps_short = bell_draw(seeds[7], (SHORT, SLAB), 0.4, 2.0, ((1, 4),), jnp.float32)
    skip_short = bell_draw(seeds[8], (SLAB,), 1.0, 4.0, ((0, 4),), jnp.float32)
    return {"token_ids": token_ids, "tables": tables, "filter_long": filter_long, "skip_long": skip_long, "taps_in": taps_in, "projection": projection, "taps_proj": taps_proj, "taps_short": taps_short, "skip_short": skip_short}


def short_filter(signal, taps):
    span = taps.shape[0]
    count = signal.shape[0]
    padded = jnp.pad(signal, [(span - 1, 0)] + [(0, 0)] * (signal.ndim - 1))
    total = jnp.zeros(signal.shape, jnp.float32)
    for offset in range(span):
        total = total + taps[offset] * padded[span - 1 - offset:span - 1 - offset + count]
    return total


def long_block(pair):
    gated_block, filter_block = pair
    length_fft = 2 * SEQ
    spectrum = jnp.fft.rfft(gated_block.astype(jnp.float32), length_fft, axis=0) * jnp.fft.rfft(filter_block.astype(jnp.float32), length_fft, axis=0)
    return jnp.fft.irfft(spectrum, length_fft, axis=0)[:SEQ].astype(jnp.bfloat16)


def reference(token_ids, tables, filter_long, skip_long, taps_in, projection, taps_proj, taps_short, skip_short):
    embedded = jnp.take(tables, token_ids, axis=0)
    features = short_filter(embedded.astype(jnp.float32), taps_in)
    query_one = features[:, 0]
    gated_one = (features[:, 1] * features[:, 2]).astype(jnp.bfloat16)
    block_width = min(WIDTH, 1024)
    blocks = WIDTH // block_width
    gated_blocks = jnp.transpose(gated_one.reshape(SEQ, blocks, block_width), (1, 0, 2))
    filter_blocks = jnp.transpose(filter_long.reshape(SEQ, blocks, block_width), (1, 0, 2))
    long_blocks = lax.map(long_block, (gated_blocks, filter_blocks))
    long_one = jnp.transpose(long_blocks, (1, 0, 2)).reshape(SEQ, WIDTH)
    layer_one = (query_one * (long_one.astype(jnp.float32) + skip_long * gated_one.astype(jnp.float32))).astype(jnp.bfloat16)
    projected = jnp.dot(layer_one, projection.reshape(WIDTH, 3 * SLAB), preferred_element_type=jnp.float32).astype(jnp.bfloat16).reshape(SEQ, 3, SLAB)
    features_two = short_filter(projected.astype(jnp.float32), taps_proj)
    gated_two = features_two[:, 1] * features_two[:, 2]
    short_two = short_filter(gated_two, taps_short)
    return (features_two[:, 0] * (short_two + skip_short * gated_two)).astype(jnp.bfloat16)
```

```python
import functools

import jax
import jax.numpy as jnp
import numpy as np
from jax import lax
from jax.experimental import pallas as pl
from jax.experimental.pallas import tpu as pltpu
from jax.sharding import PartitionSpec as P

MESH = pl.DeviceIdType.MESH
F32, BF16 = jnp.float32, jnp.bfloat16
NEAR = (0, 1, 7, 2, 6, 3, 5, 4)
SPOT = tuple(NEAR.index(k) for k in range(8))


def dft_tables():
    k1 = np.arange(64)[:, None] + 0.25
    phase = 2 * np.pi * k1 * np.arange(64)[None, :] / 64
    rows = np.concatenate([np.cos(phase), -np.sin(phase)], 0)

    def split(table):
        high = table.astype(BF16)
        return high, (table - high.astype(np.float64)).astype(BF16)

    high, low = split(rows)
    first = np.concatenate([high, low], 1)
    back_high, back_low = high.T, low.T
    last = np.concatenate([back_high, back_high, back_low], 1)
    turn = 2 * np.pi * k1 * np.arange(128)[None, :] / 8192
    inner = 2 * np.pi * np.outer(np.arange(128), np.arange(128)) / 128
    cos, sin = np.cos(inner), np.sin(inner)
    both = np.concatenate([np.concatenate([cos, -sin], 1), np.concatenate([sin, cos], 1)], 0)
    w_high, w_low = split(both)
    return (first, last, w_high, w_low, np.cos(turn).astype(np.float32), np.sin(turn).astype(np.float32))


def dot(left, right):
    return jnp.dot(left, right, preferred_element_type=F32)


def dot_t(left, right):
    return lax.dot_general(left, right, (((1,), (1,)), ((), ())), preferred_element_type=F32)


def halves(value):
    high = value.astype(BF16)
    return high, (value - high.astype(F32)).astype(BF16)


def kernel(
    tok_ref, tab_ref, filt_ref, tin_ref, proj_ref, tout_ref,
    first_ref, last_ref, wh_ref, wl_ref, cos_ref, sin_ref,
    out_ref,
    tok_all, tab_buf, tab_t, tin_t, filt_t, filt_z, filt_x, filt_f, gated, query, long_f,
    spec, send_a, all_a, b_half, b_all, c_send, c_recv, c_mine, y_send, y_recv,
    taps_mine, halo_send, halo_recv, out_send, out_recv,
    tab_sem, tz_s, tz_r, tx_s, tx_r, fz_s, fz_r, fx_s, fx_r, sw_s, sw_r, bp_s, bm_s, b_r,
    az_s, az_r, ax_s, ax_r, cc_s, cc_r, cy_s, cy_r, tp_s, tp_r, h_s, h_r, o_s, o_r,
):
    ctx, ch = lax.axis_index("ctx"), lax.axis_index("ch")
    x, yl, z = ctx // 16, (ctx // 8) % 2, ctx % 8
    yh, core = ch // 2, ch % 2
    xy = x * 2 + yl
    y = yh * 2 + yl

    def dev(x_, yl_, z_, ch_):
        return {"ctx": x_ * 16 + yl_ * 8 + z_, "ch": ch_}

    def z_peer(k):
        return dev(x, yl, lax.rem(z + k, 8), ch)

    def xy_peer(k):
        other = lax.rem(xy + k, 8)
        return dev(other // 2, other % 2, z, ch)

    def x_peer(k):
        return dev(lax.rem(x + k, 4), yl, z, ch)

    core_peer = dev(x, yl, z, yh * 2 + 1 - core)

    def y_peer(k):
        other = lax.rem(y + k, 4)
        return dev(x, other % 2, z, (other // 2) * 2 + core)

    turned = dev(ch, yl, z, x)
    is_turned = x != ch
    place = ch * 16 + yl * 8 + z

    def owner(index):
        return dev(x, (index // 8) % 2, index % 8, index // 16)

    has_next, has_prev = place < 63, place > 0

    def remote(src, dst, send, recv, device):
        return pltpu.make_async_remote_copy(
            src_ref=src, dst_ref=dst, send_sem=send, recv_sem=recv, device_id=device, device_id_type=MESH
        )

    bar = pltpu.get_barrier_semaphore()

    def greet(device):
        pl.semaphore_signal(bar, inc=1, device_id=device, device_id_type=MESH)

    for k in range(1, 8):
        greet(z_peer(k))
        greet(xy_peer(k))
    greet(dev(x, yl, z, (1 - yh) * 2 + core))
    greet(dev(x, 1 - yl, z, (1 - yh) * 2 + core))
    greet(core_peer)
    pl.when(is_turned)(lambda: greet(turned))
    pl.when((z == 7) & has_next)(lambda: greet(owner(place + 1)))
    pl.when((z == 0) & has_prev)(lambda: greet(owner(place - 1)))

    lanes = pl.multiple_of((ctx // 4) * 128, 128)
    tab_copy = pltpu.make_async_copy(tab_ref.at[:, :, pl.ds(lanes, 128)], tab_buf, tab_sem)
    tab_copy.start()
    for group in range(16):
        block = filt_ref[:, group * 128 : (group + 1) * 128].T
        for part in range(4):
            index = group * 4 + part
            filt_t[index // 8, index % 8] = block[part * 32 : (part + 1) * 32]
    for half in range(2):
        for part in range(4):
            start = part * 512 + half * 256
            b_half[half, :, :, part * 256 : (part + 1) * 256] = proj_ref[:, :, start : start + 256]
    tok_all[ctx] = tok_ref[...]
    tin_t[...] = tin_ref[:, pl.ds(lanes, 128)].T
    rows = pl.multiple_of((ctx % 4) * 32, 32)
    tin = tin_t[pl.ds(rows, 32), :]

    expected = 17 + jnp.where(is_turned, 1, 0)
    expected += jnp.where((z == 7) & has_next, 1, 0) + jnp.where((z == 0) & has_prev, 1, 0)
    pl.semaphore_wait(bar, expected)

    def tok_z(k):
        return remote(tok_all.at[ctx], tok_all.at[ctx], tz_s.at[k], tz_r.at[k], z_peer(k))

    def filt_along_z(k):
        return remote(
            filt_t.at[:, lax.rem(z + k, 8)], filt_z.at[:, SPOT[k]], fz_s.at[k], fz_r.at[k], z_peer(k)
        )

    for k in range(1, 8):
        tok_z(k).start()
    for k in NEAR[1:]:
        filt_along_z(k).start()
    swap = remote(b_half.at[1 - yl], b_all.at[:, yl, z], sw_s, sw_r, dev(x, 1 - yl, z, ch))
    swap.start()
    taps_copy = remote(tout_ref, taps_mine, tp_s, tp_r, turned)
    pl.when(is_turned)(lambda: taps_copy.start())

    @pl.when(x == ch)
    def _():
        taps_mine[...] = tout_ref[...]

    b_all[:, yl, z] = b_half[yl]
    for other in range(8):
        filt_z[other, 0] = filt_t[other, z]
    tab_copy.wait()
    for j in range(3):
        tab_t[...] = tab_buf[j].T
        spec[pl.ds(32 * j, 32), 0:512] = tab_t[pl.ds(rows, 32), :].astype(F32)
    table = spec[0:96, 0:512].astype(BF16)

    def tok_x(k):
        line = tok_all.at[pl.ds(xy * 8, 8)]
        return remote(line, line, tx_s.at[k], tx_r.at[k], xy_peer(k))

    for k in range(1, 8):
        tok_z(k).wait()
    for k in range(1, 8):
        tok_x(k).start()

    def filt_over_x(wave, k):
        spots = pl.ds(0, 5) if wave == 0 else pl.ds(5, 3)
        other = lax.rem(xy + k, 8)
        return remote(
            filt_z.at[other, spots], filt_x.at[xy, spots], fx_s.at[wave, k], fx_r.at[wave, k], xy_peer(k)
        )

    for k in range(1, 8):
        tok_x(k).wait()

    def embed(chunk, carry):
        ids = jnp.concatenate([tok_all[chunk * 4 + i] for i in range(4)], 1)
        hot = (lax.broadcasted_iota(jnp.int32, (512, 512), 0) == ids).astype(F32).astype(BF16)
        value = dot(table, hot)
        wide = jnp.concatenate([carry, value], 1)
        total = None
        parts = []
        for j in range(3):
            total = tin[:, j : j + 1] * value[32 * j : 32 * j + 32]
            for s in (1, 2):
                moved = pltpu.roll(wide[32 * j : 32 * j + 32], s, 1)[:, 128:]
                total = total + tin[:, 3 * s + j : 3 * s + j + 1] * moved
            parts.append(total)
        gate = (parts[1] * parts[2]).astype(BF16).astype(F32)
        for i in range(4):
            at = pl.ds(pl.multiple_of((chunk * 4 + i) * 32, 32), 32)
            gated[at, :] = gate[:, i * 128 : (i + 1) * 128]
            query[at, :] = parts[0][:, i * 128 : (i + 1) * 128]
        return value[:, 384:]

    carry = lax.fori_loop(0, 8, embed, jnp.zeros((96, 128), F32))
    for k in NEAR[1:5]:
        filt_along_z(k).wait()
    for k in range(1, 8):
        filt_over_x(0, k).start()
    carry = lax.fori_loop(8, 16, embed, carry)
    for k in NEAR[5:]:
        filt_along_z(k).wait()
    for k in range(1, 8):
        filt_over_x(1, k).start()
    filt_x[xy] = filt_z[xy]

    def ring(direction, step):
        which = lax.rem(z + (8 - step if direction > 0 else step), 8)
        chunk = b_all.at[:, :, which]
        sems = (bp_s if direction > 0 else bm_s).at[step]
        return remote(chunk, chunk, sems, b_r.at[direction, step], z_peer(1 if direction > 0 else 7))

    swap.wait()
    ring(1, 0).start()
    ring(0, 0).start()

    def forward(source, group):
        columns = [source[pl.ds(group * 4 + i, 64, stride=32), :] for i in range(4)]
        column = jnp.concatenate(columns, 1).astype(BF16)
        stage = dot(first_ref[...], jnp.concatenate([column, column], 0))
        cos, sin = cos_ref[...], sin_ref[...]
        turned_rows = []
        for i in range(4):
            re, im = stage[:64, i * 128 : (i + 1) * 128], stage[64:, i * 128 : (i + 1) * 128]
            turned_rows.append(jnp.concatenate([re * cos + im * sin, im * cos - re * sin], 1))
        high, low = halves(jnp.concatenate(turned_rows, 0))
        return dot(high, wh_ref[...]) + (dot(low, wh_ref[...]) + dot(high, wl_ref[...]))

    def signal_side(group, _):
        spec[pl.ds(pl.multiple_of(group * 256, 256), 256), 0:256] = forward(gated, group)
        return 0

    lax.fori_loop(0, 8, signal_side, 0)
    for wave in range(2):
        for k in range(1, 8):
            filt_over_x(wave, k).wait()
    for step in range(3):
        ring(1, step).wait()
        ring(1, step + 1).start()
        ring(0, step).wait()
        if step < 2:
            ring(0, step + 1).start()
    for other in range(8):
        for spot in range(8):
            from_z = lax.rem(z + 8 - NEAR[spot], 8)
            at = pl.ds(pl.multiple_of((other * 8 + from_z) * 32, 32), 32)
            filt_f[at, :] = filt_x[other, spot].astype(F32)

    def filter_side(group, _):
        h = forward(filt_f, group)
        s = spec[pl.ds(pl.multiple_of(group * 256, 256), 256), 0:256]
        sr, si, hr, hi = s[:, :128], s[:, 128:], h[:, :128], h[:, 128:]
        high, low = halves(jnp.concatenate([sr * hr - si * hi, sr * hi + si * hr], 1))
        back = dot_t(high, wh_ref[...]) + (dot_t(low, wh_ref[...]) + dot_t(high, wl_ref[...]))
        cos, sin = cos_ref[...], sin_ref[...]
        parts = []
        for i in range(4):
            re, im = back[i * 64 : (i + 1) * 64, :128], back[i * 64 : (i + 1) * 64, 128:]
            parts.append(jnp.concatenate([re * cos - im * sin, im * cos + re * sin], 0))
        high, low = halves(jnp.concatenate(parts, 1))
        result = dot(last_ref[...], jnp.concatenate([high, low, high], 0)) * (1.0 / 8192)
        for i in range(4):
            long_f[pl.ds(group * 4 + i, 64, stride=32), :] = result[:, i * 128 : (i + 1) * 128]
        return 0

    lax.fori_loop(0, 8, filter_side, 0)

    skip = jnp.broadcast_to(tin[:, 9:10], (32, 128))
    for index in range(64):
        x_, yl_, z_ = index // 16, (index // 8) % 2, index % 8
        at = pl.ds(index * 32, 32)
        rounded = long_f[at, :].astype(BF16).astype(F32)
        value = (query[at, :] * (rounded + skip * gated[at, :])).astype(BF16)
        send_a[(x_ // 2) * 2 + yl_, x_ % 2, z_] = value

    order = [lax.rem(y + off, 4) for off in (2, 1, 3, 0)]

    def a_z(t, k):
        q = order[t]
        return remote(
            send_a.at[q, :, lax.rem(z + k, 8)], all_a.at[x, q, :, z], az_s.at[t, k], az_r.at[t, k], z_peer(k)
        )

    def a_x(t, k):
        mine = all_a.at[x, order[t]]
        return remote(mine, mine, ax_s.at[t, k], ax_r.at[t, k], x_peer(k))

    for t in range(4):
        for k in NEAR[1:]:
            a_z(t, k).start()
        all_a[x, order[t], :, z] = send_a[order[t], :, z]
    ring(1, 3).wait()

    def c_core(t):
        return remote(c_send.at[t], c_recv.at[t], cc_s.at[t], cc_r.at[t], core_peer)

    def c_y(t):
        return remote(y_send.at[t], y_recv.at[t], cy_s.at[t], cy_r.at[t], y_peer((2, 1, 3)[t]))

    def after_core(t):
        c_core(t).wait()
        total = c_mine[t] + c_recv[t].astype(F32)
        if t < 3:
            y_send[t] = total.astype(BF16)
            c_y(t).start()
        else:
            c_mine[t] = total

    for t in range(4):
        for k in NEAR[1:]:
            a_z(t, k).wait()
        for k in range(1, 4):
            a_x(t, k).start()
    for t in range(4):
        for k in range(1, 4):
            a_x(t, k).wait()

        def columns(part, _):
            at = pl.ds(pl.multiple_of(part * 256, 256), 256)
            total = None
            for xs in range(4):
                blocks = [all_a[xs, order[t], lo].reshape(256, 128) for lo in range(2)]
                weights = b_all[part].reshape(256, 1024)[:, xs * 256 : (xs + 1) * 256]
                term = dot(weights, jnp.concatenate(blocks, 1))
                total = term if total is None else total + term
            @pl.when(core == 0)
            def _():
                c_mine[t, at, :] = total[:, :128]
                c_send[t, at, :] = total[:, 128:].astype(BF16)

            @pl.when(core == 1)
            def _():
                c_mine[t, at, :] = total[:, 128:]
                c_send[t, at, :] = total[:, :128].astype(BF16)

            return 0

        lax.fori_loop(0, 3, columns, 0)
        c_core(t).start()
        if t > 0:
            after_core(t - 1)
    after_core(3)
    for t in range(3):
        c_y(t).wait()
    summed = c_mine[3] + y_recv[0].astype(F32) + y_recv[1].astype(F32) + y_recv[2].astype(F32)
    projected = jnp.concatenate([summed[i * 128 : (i + 1) * 128].T for i in range(6)], 1).astype(BF16)

    halo = remote(halo_send, halo_recv, h_s, h_r, owner(place + 1))
    halo_send[...] = projected[112:]
    pl.when(has_next)(lambda: halo.start())

    @pl.when(place == 0)
    def _():
        halo_recv[...] = jnp.zeros_like(halo_recv)

    pl.when(has_next)(lambda: halo.wait_send())
    pl.when(has_prev)(lambda: halo.wait_recv())
    pl.when(is_turned)(lambda: taps_copy.wait())
    wide = jnp.concatenate([halo_recv[...], projected], 0).astype(F32)

    def shifted(value, s):
        return value if s == 0 else pltpu.roll(value, s, 0)

    feats = []
    for j in range(3):
        part = wide[:, j * 256 : (j + 1) * 256]
        total = None
        for s in range(3):
            term = taps_mine[3 * s + j : 3 * s + j + 1, :] * shifted(part, s)
            total = term if total is None else total + term
        feats.append(total)
    gate = feats[1] * feats[2]
    short = None
    for s in range(7):
        term = taps_mine[9 + s : 10 + s, :] * shifted(gate, s)
        short = term if short is None else short + term
    mixed = (feats[0] * (short + taps_mine[16:17, :] * gate))[16:].astype(BF16)

    out_send[...] = mixed
    out_copy = remote(out_send, out_recv, o_s, o_r, turned)

    @pl.when(is_turned)
    def _():
        out_copy.start()
        out_copy.wait()

    @pl.when(x == ch)
    def _():
        out_recv[...] = out_send[...]

    out_ref[...] = out_recv[...]


def per_device(token_ids, tables, filter_long, skip_long, taps_in, projection, taps_proj, taps_short, skip_short):
    tin = jnp.concatenate([taps_in.reshape(9, 2048), skip_long[None], jnp.zeros((6, 2048), F32)], 0)
    tout = jnp.concatenate(
        [taps_proj.reshape(9, 256), taps_short, skip_short[None], jnp.zeros((7, 256), F32)], 0
    )
    vmem = pl.BlockSpec(memory_space=pltpu.VMEM)
    dma = pltpu.SemaphoreType.DMA
    scratch = [
        pltpu.VMEM((64, 1, 128), jnp.int32),
        pltpu.VMEM((3, 512, 128), BF16),
        pltpu.VMEM((128, 512), BF16),
        pltpu.VMEM((128, 16), F32),
        pltpu.VMEM((8, 8, 32, 128), BF16),
        pltpu.VMEM((8, 8, 32, 128), BF16),
        pltpu.VMEM((8, 8, 32, 128), BF16),
        pltpu.VMEM((2048, 128), F32),
        pltpu.VMEM((2048, 128), F32),
        pltpu.VMEM((2048, 128), F32),
        pltpu.VMEM((2048, 128), F32),
        pltpu.VMEM((2048, 512), F32),
        pltpu.VMEM((4, 2, 8, 32, 128), BF16),
        pltpu.VMEM((4, 4, 2, 8, 32, 128), BF16),
        pltpu.VMEM((2, 3, 16, 1024), BF16),
        pltpu.VMEM((3, 2, 8, 16, 1024), BF16),
        pltpu.VMEM((4, 768, 128), BF16),
        pltpu.VMEM((4, 768, 128), BF16),
        pltpu.VMEM((4, 768, 128), F32),
        pltpu.VMEM((3, 768, 128), BF16),
        pltpu.VMEM((3, 768, 128), BF16),
        pltpu.VMEM((24, 256), F32),
        pltpu.VMEM((16, 768), BF16),
        pltpu.VMEM((16, 768), BF16),
        pltpu.VMEM((128, 256), BF16),
        pltpu.VMEM((128, 256), BF16),
        dma, dma((8,)), dma((8,)), dma((8,)), dma((8,)),
        dma((8,)), dma((8,)), dma((2, 8)), dma((2, 8)),
        dma, dma, dma((4,)), dma((4,)), dma((2, 4)),
        dma((4, 8)), dma((4, 8)), dma((4, 4)), dma((4, 4)),
        dma((4,)), dma((4,)), dma((3,)), dma((3,)),
        dma, dma, dma, dma, dma, dma,
    ]
    return pl.pallas_call(
        kernel,
        out_shape=jax.ShapeDtypeStruct((128, 256), BF16),
        in_specs=[vmem, pl.BlockSpec(memory_space=pl.ANY)] + [vmem] * 10,
        out_specs=vmem,
        scratch_shapes=scratch,
        compiler_params=pltpu.CompilerParams(
            collective_id=0, has_side_effects=True, vmem_limit_bytes=48 * 2**20
        ),
    )(
        token_ids.reshape(1, 128), jnp.transpose(tables, (1, 0, 2)), filter_long, tin,
        jnp.transpose(projection, (1, 2, 0)), tout, *[jnp.asarray(t) for t in dft_tables()],
    )


def solution(mesh):
    placed = (
        P("ctx"),
        P(None, None, "ch"),
        P("ctx", "ch"),
        P("ch"),
        P(None, None, "ch"),
        P("ch", None, "ctx"),
        P(None, None, "ch"),
        P(None, "ch"),
        P("ch"),
    )
    return jax.shard_map(
        per_device, mesh=mesh, in_specs=placed, out_specs=P("ctx", "ch"), check_vma=False
    )
```

```python
import functools

import jax
import jax.numpy as jnp
import numpy as np
from jax import lax
from jax.experimental import pallas as pl
from jax.experimental.pallas import tpu as pltpu
from jax.sharding import PartitionSpec as P

MESH = pl.DeviceIdType.MESH
F32, BF16 = jnp.float32, jnp.bfloat16
NEAR = (0, 1, 7, 2, 6, 3, 5, 4)
SPOT = tuple(NEAR.index(k) for k in range(8))


def dft_tables():
    k1 = np.arange(64)[:, None] + 0.25
    phase = 2 * np.pi * k1 * np.arange(64)[None, :] / 64
    rows = np.concatenate([np.cos(phase), -np.sin(phase)], 0)

    def split(table):
        high = table.astype(BF16)
        return high, (table - high.astype(np.float64)).astype(BF16)

    high, low = split(rows)
    first = np.concatenate([high, low], 1)
    back_high, back_low = high.T, low.T
    last = np.concatenate([back_high, back_high, back_low], 1)
    turn = 2 * np.pi * k1 * np.arange(128)[None, :] / 8192
    inner = 2 * np.pi * np.outer(np.arange(128), np.arange(128)) / 128
    cos, sin = np.cos(inner), np.sin(inner)
    both = np.concatenate([np.concatenate([cos, -sin], 1), np.concatenate([sin, cos], 1)], 0)
    w_high, w_low = split(both)
    tall = [first, *np.split(last, 3, 1), *np.split(w_high, 2, 1), *np.split(w_low, 2, 1)]
    return np.concatenate(tall, 0), np.concatenate([np.cos(turn), np.sin(turn)], 0).astype(np.float32)


def dot(left, right):
    return jnp.dot(left, right, preferred_element_type=F32)


def dot_t(left, right):
    return lax.dot_general(left, right, (((1,), (1,)), ((), ())), preferred_element_type=F32)


def halves(value):
    high = value.astype(BF16)
    return high, (value - high.astype(F32)).astype(BF16)


def kernel(
    tok_hbm, tab_hbm, filt_hbm, tin_hbm, skip_hbm, proj_hbm, tpr_hbm, tsh_hbm, ssk_hbm,
    dft_hbm, turn_hbm,
    out_ref,
    tok_ref, filt_ref, tin_ref, skip_ref, proj_ref, tpr_ref, tsh_ref, ssk_ref,
    dft_ref, turn_ref, tout_ref, load_sem,
    tok_all, tab_buf, tab_t, tin_t, filt_t, filt_z, filt_x, filt_f, gated, query, long_f,
    spec, send_a, all_a, b_half, b_all, c_send, c_recv, c_mine, y_send, y_recv,
    taps_mine, halo_send, halo_recv, out_send, out_recv,
    tab_sem, tz_s, tz_r, tx_s, tx_r, fz_s, fz_r, fx_s, fx_r, sw_s, sw_r, bp_s, bm_s, b_r,
    az_s, az_r, ax_s, ax_r, cc_s, cc_r, cy_s, cy_r, tp_s, tp_r, h_s, h_r, o_s, o_r,
):
    ctx, ch = lax.axis_index("ctx"), lax.axis_index("ch")
    x, yl, z = ctx // 16, (ctx // 8) % 2, ctx % 8
    yh, core = ch // 2, ch % 2
    xy = x * 2 + yl
    y = yh * 2 + yl

    def dev(x_, yl_, z_, ch_):
        return {"ctx": x_ * 16 + yl_ * 8 + z_, "ch": ch_}

    def z_peer(k):
        return dev(x, yl, lax.rem(z + k, 8), ch)

    def xy_peer(k):
        other = lax.rem(xy + k, 8)
        return dev(other // 2, other % 2, z, ch)

    def x_peer(k):
        return dev(lax.rem(x + k, 4), yl, z, ch)

    core_peer = dev(x, yl, z, yh * 2 + 1 - core)

    def y_peer(k):
        other = lax.rem(y + k, 4)
        return dev(x, other % 2, z, (other // 2) * 2 + core)

    turned = dev(ch, yl, z, x)
    is_turned = x != ch
    place = ch * 16 + yl * 8 + z

    def owner(index):
        return dev(x, (index // 8) % 2, index % 8, index // 16)

    has_next, has_prev = place < 63, place > 0

    def remote(src, dst, send, recv, device):
        return pltpu.make_async_remote_copy(
            src_ref=src, dst_ref=dst, send_sem=send, recv_sem=recv, device_id=device, device_id_type=MESH
        )

    lanes = pl.multiple_of((ctx // 4) * 128, 128)
    tab_copy = pltpu.make_async_copy(tab_hbm.at[:, :, pl.ds(lanes, 128)], tab_buf, tab_sem)
    pairs = (
        (filt_hbm, filt_ref), (tok_hbm, tok_ref), (proj_hbm, proj_ref), (tin_hbm, tin_ref),
        (skip_hbm, skip_ref), (tpr_hbm, tpr_ref), (tsh_hbm, tsh_ref), (ssk_hbm, ssk_ref),
        (dft_hbm, dft_ref), (turn_hbm, turn_ref),
    )
    loads = [pltpu.make_async_copy(src, dst, load_sem.at[i]) for i, (src, dst) in enumerate(pairs)]
    for load in loads:
        load.start()
    tab_copy.start()

    bar = pltpu.get_barrier_semaphore()

    def greet(device):
        pl.semaphore_signal(bar, inc=1, device_id=device, device_id_type=MESH)

    for k in range(1, 8):
        greet(z_peer(k))
        greet(xy_peer(k))
    greet(dev(x, yl, z, (1 - yh) * 2 + core))
    greet(dev(x, 1 - yl, z, (1 - yh) * 2 + core))
    greet(core_peer)
    pl.when(is_turned)(lambda: greet(turned))
    pl.when((z == 7) & has_next)(lambda: greet(owner(place + 1)))
    pl.when((z == 0) & has_prev)(lambda: greet(owner(place - 1)))

    loads[0].wait()
    for group in range(16):
        block = filt_ref[:, group * 128 : (group + 1) * 128].T
        for part in range(4):
            index = group * 4 + part
            filt_t[index // 8, index % 8] = block[part * 32 : (part + 1) * 32]
    for load in loads[1:]:
        load.wait()
    for half in range(2):
        for part in range(4):
            start = part * 512 + half * 256
            b_half[half, :, :, part * 256 : (part + 1) * 256] = proj_ref[:, :, start : start + 256]
    tok_all[ctx] = tok_ref[...]
    stacked = [tin_ref[s, :, pl.ds(lanes, 128)] for s in range(3)] + [skip_ref[pl.ds(ctx // 4, 1), :]]
    tin_t[...] = jnp.concatenate(stacked + [jnp.zeros((6, 128), F32)], 0).T
    for s in range(3):
        tout_ref[3 * s : 3 * s + 3, :] = tpr_ref[s]
    tout_ref[9:16, :] = tsh_ref[...]
    tout_ref[16:17, :] = jnp.concatenate([ssk_ref[0:1, :], ssk_ref[1:2, :]], 1)
    tout_ref[17:24, :] = jnp.zeros((7, 256), F32)
    rows = pl.multiple_of((ctx % 4) * 32, 32)
    tin = tin_t[pl.ds(rows, 32), :]

    expected = 17 + jnp.where(is_turned, 1, 0)
    expected += jnp.where((z == 7) & has_next, 1, 0) + jnp.where((z == 0) & has_prev, 1, 0)
    pl.semaphore_wait(bar, expected)

    def tok_z(k):
        return remote(tok_all.at[ctx], tok_all.at[ctx], tz_s.at[k], tz_r.at[k], z_peer(k))

    def filt_along_z(k):
        return remote(
            filt_t.at[:, lax.rem(z + k, 8)], filt_z.at[:, SPOT[k]], fz_s.at[k], fz_r.at[k], z_peer(k)
        )

    for k in range(1, 8):
        tok_z(k).start()
    for k in NEAR[1:]:
        filt_along_z(k).start()
    swap = remote(b_half.at[1 - yl], b_all.at[:, yl, z], sw_s, sw_r, dev(x, 1 - yl, z, ch))
    swap.start()
    taps_copy = remote(tout_ref, taps_mine, tp_s, tp_r, turned)
    pl.when(is_turned)(lambda: taps_copy.start())

    @pl.when(x == ch)
    def _():
        taps_mine[...] = tout_ref[...]

    b_all[:, yl, z] = b_half[yl]
    for other in range(8):
        filt_z[other, 0] = filt_t[other, z]
    tab_copy.wait()
    for j in range(3):
        tab_t[...] = tab_buf[j].T
        spec[pl.ds(32 * j, 32), 0:512] = tab_t[pl.ds(rows, 32), :].astype(F32)
    table = spec[0:96, 0:512].astype(BF16)

    def tok_x(k):
        line = tok_all.at[pl.ds(xy * 8, 8)]
        return remote(line, line, tx_s.at[k], tx_r.at[k], xy_peer(k))

    for k in range(1, 8):
        tok_z(k).wait()
    for k in range(1, 8):
        tok_x(k).start()

    def filt_over_x(wave, k):
        spots = pl.ds(0, 5) if wave == 0 else pl.ds(5, 3)
        other = lax.rem(xy + k, 8)
        return remote(
            filt_z.at[other, spots], filt_x.at[xy, spots], fx_s.at[wave, k], fx_r.at[wave, k], xy_peer(k)
        )

    for k in range(1, 8):
        tok_x(k).wait()

    def embed(chunk, carry):
        ids = jnp.concatenate([tok_all[chunk * 4 + i] for i in range(4)], 1)
        hot = (lax.broadcasted_iota(jnp.int32, (512, 512), 0) == ids).astype(F32).astype(BF16)
        value = dot(table, hot)
        wide = jnp.concatenate([carry, value], 1)
        total = None
        parts = []
        for j in range(3):
            total = tin[:, j : j + 1] * value[32 * j : 32 * j + 32]
            for s in (1, 2):
                moved = pltpu.roll(wide[32 * j : 32 * j + 32], s, 1)[:, 128:]
                total = total + tin[:, 3 * s + j : 3 * s + j + 1] * moved
            parts.append(total)
        gate = (parts[1] * parts[2]).astype(BF16).astype(F32)
        for i in range(4):
            at = pl.ds(pl.multiple_of((chunk * 4 + i) * 32, 32), 32)
            gated[at, :] = gate[:, i * 128 : (i + 1) * 128]
            query[at, :] = parts[0][:, i * 128 : (i + 1) * 128]
        return value[:, 384:]

    carry = lax.fori_loop(0, 8, embed, jnp.zeros((96, 128), F32))
    for k in NEAR[1:5]:
        filt_along_z(k).wait()
    for k in range(1, 8):
        filt_over_x(0, k).start()
    carry = lax.fori_loop(8, 16, embed, carry)
    for k in NEAR[5:]:
        filt_along_z(k).wait()
    for k in range(1, 8):
        filt_over_x(1, k).start()
    filt_x[xy] = filt_z[xy]

    def ring(direction, step):
        which = lax.rem(z + (8 - step if direction > 0 else step), 8)
        chunk = b_all.at[:, :, which] if step < 3 else b_all.at[:, 0 if direction > 0 else 1, which]
        sems = (bp_s if direction > 0 else bm_s).at[step]
        return remote(chunk, chunk, sems, b_r.at[direction, step], z_peer(1 if direction > 0 else 7))

    def ring_on(step):
        for direction in (1, 0):
            ring(direction, step).wait()
            if step < 3:
                ring(direction, step + 1).start()

    swap.wait()
    ring(1, 0).start()
    ring(0, 0).start()

    def first():
        return dft_ref[0:128, :]

    def last():
        return jnp.concatenate([dft_ref[128 + 64 * i : 192 + 64 * i, :] for i in range(3)], 1)

    def w_high():
        return jnp.concatenate([dft_ref[320:576, :], dft_ref[576:832, :]], 1)

    def w_low():
        return jnp.concatenate([dft_ref[832:1088, :], dft_ref[1088:1344, :]], 1)

    def turns():
        return turn_ref[0:64, :], turn_ref[64:128, :]

    def forward(source, group):
        columns = [source[pl.ds(group * 4 + i, 64, stride=32), :] for i in range(4)]
        column = jnp.concatenate(columns, 1).astype(BF16)
        stage = dot(first(), jnp.concatenate([column, column], 0))
        cos, sin = turns()
        turned_rows = []
        for i in range(4):
            re, im = stage[:64, i * 128 : (i + 1) * 128], stage[64:, i * 128 : (i + 1) * 128]
            turned_rows.append(jnp.concatenate([re * cos + im * sin, im * cos - re * sin], 1))
        high, low = halves(jnp.concatenate(turned_rows, 0))
        return dot(high, w_high()) + (dot(low, w_high()) + dot(high, w_low()))

    def signal_side(group, _):
        spec[pl.ds(pl.multiple_of(group * 256, 256), 256), 0:256] = forward(gated, group)
        return 0

    lax.fori_loop(0, 8, signal_side, 0)
    for k in range(1, 8):
        filt_over_x(0, k).wait()
    ring_on(0)
    for k in range(1, 8):
        filt_over_x(1, k).wait()
    for other in range(8):
        for spot in range(8):
            from_z = lax.rem(z + 8 - NEAR[spot], 8)
            at = pl.ds(pl.multiple_of((other * 8 + from_z) * 32, 32), 32)
            filt_f[at, :] = filt_x[other, spot].astype(F32)

    def filter_side(group, _):
        h = forward(filt_f, group)
        s = spec[pl.ds(pl.multiple_of(group * 256, 256), 256), 0:256]
        sr, si, hr, hi = s[:, :128], s[:, 128:], h[:, :128], h[:, 128:]
        high, low = halves(jnp.concatenate([sr * hr - si * hi, sr * hi + si * hr], 1))
        back = dot_t(high, w_high()) + (dot_t(low, w_high()) + dot_t(high, w_low()))
        cos, sin = turns()
        parts = []
        for i in range(4):
            re, im = back[i * 64 : (i + 1) * 64, :128], back[i * 64 : (i + 1) * 64, 128:]
            parts.append(jnp.concatenate([re * cos - im * sin, im * cos + re * sin], 0))
        high, low = halves(jnp.concatenate(parts, 1))
        result = dot(last(), jnp.concatenate([high, low, high], 0)) * (1.0 / 8192)
        for i in range(4):
            long_f[pl.ds(group * 4 + i, 64, stride=32), :] = result[:, i * 128 : (i + 1) * 128]
        return 0

    lax.fori_loop(0, 8, filter_side, 0)

    skip = jnp.broadcast_to(tin[:, 9:10], (32, 128))
    for index in range(64):
        x_, yl_, z_ = index // 16, (index // 8) % 2, index % 8
        at = pl.ds(index * 32, 32)
        rounded = long_f[at, :].astype(BF16).astype(F32)
        value = (query[at, :] * (rounded + skip * gated[at, :])).astype(BF16)
        send_a[(x_ // 2) * 2 + yl_, x_ % 2, z_] = value

    order = [lax.rem(y + off, 4) for off in (2, 1, 3, 0)]

    def a_z(t, k):
        q = order[t]
        return remote(
            send_a.at[q, :, lax.rem(z + k, 8)], all_a.at[x, q, :, z], az_s.at[t, k], az_r.at[t, k], z_peer(k)
        )

    def a_x(t, right):
        mine = all_a.at[x, order[t]]
        return remote(mine, mine, ax_s.at[t, right], ax_r.at[t, right], x_peer(1 if right else 3))

    def a_on(t, right):
        half = all_a.at[lax.rem(x + (3 if right else 1), 4), order[t], right]
        return remote(half, half, ax_s.at[t, 2 + right], ax_r.at[t, 2 + right], x_peer(1 if right else 3))

    def pass_on(t):
        for right in (1, 0):
            a_x(t, right).wait()
            a_on(t, right).start()

    for t in range(4):
        for k in NEAR[1:]:
            a_z(t, k).start()
        all_a[x, order[t], :, z] = send_a[order[t], :, z]
    ring_on(1)

    def c_core(t):
        return remote(c_send.at[t], c_recv.at[t], cc_s.at[t], cc_r.at[t], core_peer)

    def c_y(t):
        return remote(y_send.at[t], y_recv.at[t], cy_s.at[t], cy_r.at[t], y_peer((2, 1, 3)[t]))

    def after_core(t):
        c_core(t).wait()
        total = c_mine[t] + c_recv[t].astype(F32)
        if t < 3:
            y_send[t] = total.astype(BF16)
            c_y(t).start()
        else:
            c_mine[t] = total

    for t in range(4):
        for k in NEAR[1:]:
            a_z(t, k).wait()
        for right in (1, 0):
            a_x(t, right).start()
        if t > 0:
            pass_on(t - 1)
    ring_on(2)
    pass_on(3)
    ring_on(3)
    for t in range(4):
        for right in (1, 0):
            a_on(t, right).wait()

        def columns(part, _):
            at = pl.ds(pl.multiple_of(part * 256, 256), 256)
            total = None
            for xs in range(4):
                blocks = [all_a[xs, order[t], lo].reshape(256, 128) for lo in range(2)]
                weights = b_all[part].reshape(256, 1024)[:, xs * 256 : (xs + 1) * 256]
                term = dot(weights, jnp.concatenate(blocks, 1))
                total = term if total is None else total + term
            @pl.when(core == 0)
            def _():
                c_mine[t, at, :] = total[:, :128]
                c_send[t, at, :] = total[:, 128:].astype(BF16)

            @pl.when(core == 1)
            def _():
                c_mine[t, at, :] = total[:, 128:]
                c_send[t, at, :] = total[:, :128].astype(BF16)

            return 0

        lax.fori_loop(0, 3, columns, 0)
        c_core(t).start()
        if t > 0:
            after_core(t - 1)
    after_core(3)
    for t in range(3):
        c_y(t).wait()
    summed = c_mine[3] + y_recv[0].astype(F32) + y_recv[1].astype(F32) + y_recv[2].astype(F32)
    projected = jnp.concatenate([summed[i * 128 : (i + 1) * 128].T for i in range(6)], 1).astype(BF16)

    halo = remote(halo_send, halo_recv, h_s, h_r, owner(place + 1))
    halo_send[...] = projected[112:]
    pl.when(has_next)(lambda: halo.start())

    @pl.when(place == 0)
    def _():
        halo_recv[...] = jnp.zeros_like(halo_recv)

    pl.when(has_next)(lambda: halo.wait_send())
    pl.when(has_prev)(lambda: halo.wait_recv())
    pl.when(is_turned)(lambda: taps_copy.wait())
    wide = jnp.concatenate([halo_recv[...], projected], 0).astype(F32)

    def shifted(value, s):
        return value if s == 0 else pltpu.roll(value, s, 0)

    feats = []
    for j in range(3):
        part = wide[:, j * 256 : (j + 1) * 256]
        total = None
        for s in range(3):
            term = taps_mine[3 * s + j : 3 * s + j + 1, :] * shifted(part, s)
            total = term if total is None else total + term
        feats.append(total)
    gate = feats[1] * feats[2]
    short = None
    for s in range(7):
        term = taps_mine[9 + s : 10 + s, :] * shifted(gate, s)
        short = term if short is None else short + term
    mixed = (feats[0] * (short + taps_mine[16:17, :] * gate))[16:].astype(BF16)

    out_send[...] = mixed
    out_copy = remote(out_send, out_recv, o_s, o_r, turned)

    @pl.when(is_turned)
    def _():
        out_copy.start()
        out_copy.wait()

    @pl.when(x == ch)
    def _():
        out_recv[...] = out_send[...]

    out_ref[...] = out_recv[...]


def per_device(token_ids, tables, filter_long, skip_long, taps_in, projection, taps_proj, taps_short, skip_short):
    vmem = pl.BlockSpec(memory_space=pltpu.VMEM)
    hbm = pl.BlockSpec(memory_space=pltpu.HBM)
    tables_dft = [jnp.asarray(t) for t in dft_tables()]
    dma = pltpu.SemaphoreType.DMA
    scratch = [
        pltpu.VMEM((1, 128), jnp.int32),
        pltpu.VMEM((128, 2048), BF16),
        pltpu.VMEM((3, 3, 2048), F32),
        pltpu.VMEM((16, 128), F32),
        pltpu.VMEM((3, 16, 2048), BF16),
        pltpu.VMEM((3, 3, 256), F32),
        pltpu.VMEM((7, 256), F32),
        pltpu.VMEM((2, 128), F32),
        *[pltpu.VMEM(t.shape, t.dtype) for t in tables_dft],
        pltpu.VMEM((24, 256), F32),
        dma((10,)),
        pltpu.VMEM((64, 1, 128), jnp.int32),
        pltpu.VMEM((3, 512, 128), BF16),
        pltpu.VMEM((128, 512), BF16),
        pltpu.VMEM((128, 16), F32),
        pltpu.VMEM((8, 8, 32, 128), BF16),
        pltpu.VMEM((8, 8, 32, 128), BF16),
        pltpu.VMEM((8, 8, 32, 128), BF16),
        pltpu.VMEM((2048, 128), F32),
        pltpu.VMEM((2048, 128), F32),
        pltpu.VMEM((2048, 128), F32),
        pltpu.VMEM((2048, 128), F32),
        pltpu.VMEM((2048, 512), F32),
        pltpu.VMEM((4, 2, 8, 32, 128), BF16),
        pltpu.VMEM((4, 4, 2, 8, 32, 128), BF16),
        pltpu.VMEM((2, 3, 16, 1024), BF16),
        pltpu.VMEM((3, 2, 8, 16, 1024), BF16),
        pltpu.VMEM((4, 768, 128), BF16),
        pltpu.VMEM((4, 768, 128), BF16),
        pltpu.VMEM((4, 768, 128), F32),
        pltpu.VMEM((3, 768, 128), BF16),
        pltpu.VMEM((3, 768, 128), BF16),
        pltpu.VMEM((24, 256), F32),
        pltpu.VMEM((16, 768), BF16),
        pltpu.VMEM((16, 768), BF16),
        pltpu.VMEM((128, 256), BF16),
        pltpu.VMEM((128, 256), BF16),
        dma, dma((8,)), dma((8,)), dma((8,)), dma((8,)),
        dma((8,)), dma((8,)), dma((2, 8)), dma((2, 8)),
        dma, dma, dma((4,)), dma((4,)), dma((2, 4)),
        dma((4, 8)), dma((4, 8)), dma((4, 4)), dma((4, 4)),
        dma((4,)), dma((4,)), dma((3,)), dma((3,)),
        dma, dma, dma, dma, dma, dma,
    ]
    return pl.pallas_call(
        kernel,
        out_shape=jax.ShapeDtypeStruct((128, 256), BF16),
        in_specs=[hbm] * 11,
        out_specs=vmem,
        scratch_shapes=scratch,
        compiler_params=pltpu.CompilerParams(
            collective_id=0, has_side_effects=True, vmem_limit_bytes=60 * 2**20
        ),
    )(
        token_ids.reshape(1, 128), jnp.transpose(tables, (1, 0, 2)), filter_long, taps_in,
        skip_long.reshape(16, 128), jnp.transpose(projection, (1, 2, 0)), taps_proj, taps_short,
        skip_short.reshape(2, 128), *tables_dft,
    )


def solution(mesh):
    placed = (
        P("ctx"),
        P(None, None, "ch"),
        P("ctx", "ch"),
        P("ch"),
        P(None, None, "ch"),
        P("ch", None, "ctx"),
        P(None, None, "ch"),
        P(None, "ch"),
        P("ch"),
    )
    return jax.shard_map(
        per_device, mesh=mesh, in_specs=placed, out_specs=P("ctx", "ch"), check_vma=False
    )
```

```python
import functools

import jax
import jax.numpy as jnp
import numpy as np
from jax import lax
from jax.experimental import pallas as pl
from jax.experimental.pallas import tpu as pltpu
from jax.sharding import PartitionSpec as P

MESH = pl.DeviceIdType.MESH
F32, BF16 = jnp.float32, jnp.bfloat16
NEAR = (0, 1, 7, 2, 6, 3, 5, 4)
WAVES = (0, 5, 7, 8)
SPOT = tuple(NEAR.index(k) for k in range(8))


def dft_tables():
    k1 = np.arange(64)[:, None] + 0.25
    phase = 2 * np.pi * k1 * np.arange(64)[None, :] / 64
    rows = np.concatenate([np.cos(phase), -np.sin(phase)], 0)

    def split(table):
        high = table.astype(BF16)
        return high, (table - high.astype(np.float64)).astype(BF16)

    high, low = split(rows)
    first = np.concatenate([high, low], 1)
    turn = 2 * np.pi * k1 * np.arange(128)[None, :] / 8192
    inner = 2 * np.pi * np.outer(np.arange(128), np.arange(128)) / 128
    cos, sin = np.cos(inner), np.sin(inner)
    both = np.concatenate([np.concatenate([cos, -sin], 1), np.concatenate([sin, cos], 1)], 0)
    w_high = both.astype(BF16)
    tall = [first, high.T, low.T, *np.split(w_high, 2, 1)]
    return np.concatenate(tall, 0), np.concatenate([np.cos(turn), np.sin(turn)], 0).astype(np.float32)


def dot(left, right):
    return jnp.dot(left, right, preferred_element_type=F32)


def dot_t(left, right):
    return lax.dot_general(left, right, (((1,), (1,)), ((), ())), preferred_element_type=F32)


def kernel(
    tok_hbm, tab_hbm, filt_hbm, tin_hbm, skip_hbm, proj_hbm, tpr_hbm, tsh_hbm, ssk_hbm,
    dft_hbm, turn_hbm,
    out_ref,
    tok_ref, filt_ref, tin_ref, skip_ref, proj_ref, tpr_ref, tsh_ref, ssk_ref,
    dft_ref, turn_ref, tout_ref, load_sem,
    tok_all, tab_buf, tab_t, tin_t, filt_t, filt_z, filt_x, filt_f, gated, query, long_f,
    spec, send_a, all_a, b_half, b_all, c_send, c_recv, c_mine, y_send, y_recv,
    taps_mine, halo_send, halo_recv, out_send, out_recv,
    tab_sem, tz_s, tz_r, tx_s, tx_r, fz_s, fz_r, fx_s, fx_r, sw_s, sw_r, bp_s, bm_s, b_r,
    az_s, az_r, ax_s, ax_r, cc_s, cc_r, cy_s, cy_r, tp_s, tp_r, h_s, h_r, o_s, o_r,
):
    ctx, ch = lax.axis_index("ctx"), lax.axis_index("ch")
    x, yl, z = ctx // 16, (ctx // 8) % 2, ctx % 8
    yh, core = ch // 2, ch % 2
    xy = x * 2 + yl
    y = yh * 2 + yl

    def dev(x_, yl_, z_, ch_):
        return {"ctx": x_ * 16 + yl_ * 8 + z_, "ch": ch_}

    def z_peer(k):
        return dev(x, yl, lax.rem(z + k, 8), ch)

    def xy_peer(k):
        other = lax.rem(xy + k, 8)
        return dev(other // 2, other % 2, z, ch)

    def x_peer(k):
        return dev(lax.rem(x + k, 4), yl, z, ch)

    core_peer = dev(x, yl, z, yh * 2 + 1 - core)

    def y_peer(k):
        other = lax.rem(y + k, 4)
        return dev(x, other % 2, z, (other // 2) * 2 + core)

    turned = dev(ch, yl, z, x)
    is_turned = x != ch
    place = ch * 16 + yl * 8 + z

    def owner(index):
        return dev(x, (index // 8) % 2, index % 8, index // 16)

    has_next, has_prev = place < 63, place > 0

    def remote(src, dst, send, recv, device):
        return pltpu.make_async_remote_copy(
            src_ref=src, dst_ref=dst, send_sem=send, recv_sem=recv, device_id=device, device_id_type=MESH
        )

    lanes = pl.multiple_of((ctx // 4) * 128, 128)
    tab_copy = pltpu.make_async_copy(tab_hbm.at[:, :, pl.ds(lanes, 128)], tab_buf, tab_sem)
    pairs = (
        (filt_hbm, filt_ref), (tok_hbm, tok_ref), (proj_hbm, proj_ref), (tin_hbm, tin_ref),
        (skip_hbm, skip_ref), (tpr_hbm, tpr_ref), (tsh_hbm, tsh_ref), (ssk_hbm, ssk_ref),
        (dft_hbm, dft_ref), (turn_hbm, turn_ref),
    )
    loads = [pltpu.make_async_copy(src, dst, load_sem.at[i]) for i, (src, dst) in enumerate(pairs)]
    for load in loads:
        load.start()
    tab_copy.start()

    bar = pltpu.get_barrier_semaphore()

    def greet(device):
        pl.semaphore_signal(bar, inc=1, device_id=device, device_id_type=MESH)

    for k in range(1, 8):
        greet(z_peer(k))
        greet(xy_peer(k))
    greet(dev(x, yl, z, (1 - yh) * 2 + core))
    greet(dev(x, 1 - yl, z, (1 - yh) * 2 + core))
    greet(core_peer)
    pl.when(is_turned)(lambda: greet(turned))
    pl.when((z == 7) & has_next)(lambda: greet(owner(place + 1)))
    pl.when((z == 0) & has_prev)(lambda: greet(owner(place - 1)))

    loads[0].wait()
    for group in range(16):
        block = filt_ref[:, group * 128 : (group + 1) * 128].T
        for part in range(4):
            index = group * 4 + part
            filt_t[index // 8, index % 8] = block[part * 32 : (part + 1) * 32]
    for load in loads[1:]:
        load.wait()
    for half in range(2):
        for part in range(4):
            start = part * 512 + half * 256
            b_half[half, :, :, part * 256 : (part + 1) * 256] = proj_ref[:, :, start : start + 256]
    tok_all[ctx] = tok_ref[...]
    stacked = [tin_ref[s, :, pl.ds(lanes, 128)] for s in range(3)] + [skip_ref[pl.ds(ctx // 4, 1), :]]
    tin_t[...] = jnp.concatenate(stacked + [jnp.zeros((6, 128), F32)], 0).T
    for s in range(3):
        tout_ref[3 * s : 3 * s + 3, :] = tpr_ref[s]
    tout_ref[9:16, :] = tsh_ref[...]
    tout_ref[16:17, :] = jnp.concatenate([ssk_ref[0:1, :], ssk_ref[1:2, :]], 1)
    tout_ref[17:24, :] = jnp.zeros((7, 256), F32)
    rows = pl.multiple_of((ctx % 4) * 32, 32)
    tin = tin_t[pl.ds(rows, 32), :]

    expected = 17 + jnp.where(is_turned, 1, 0)
    expected += jnp.where((z == 7) & has_next, 1, 0) + jnp.where((z == 0) & has_prev, 1, 0)
    pl.semaphore_wait(bar, expected)

    def tok_z(k):
        return remote(tok_all.at[ctx], tok_all.at[ctx], tz_s.at[k], tz_r.at[k], z_peer(k))

    def filt_along_z(k):
        return remote(
            filt_t.at[:, lax.rem(z + k, 8)], filt_z.at[:, SPOT[k]], fz_s.at[k], fz_r.at[k], z_peer(k)
        )

    for k in range(1, 8):
        tok_z(k).start()
    for k in NEAR[1:]:
        filt_along_z(k).start()
    swap = remote(b_half.at[1 - yl], b_all.at[:, yl, z], sw_s, sw_r, dev(x, 1 - yl, z, ch))
    swap.start()
    taps_copy = remote(tout_ref, taps_mine, tp_s, tp_r, turned)
    pl.when(is_turned)(lambda: taps_copy.start())

    @pl.when(x == ch)
    def _():
        taps_mine[...] = tout_ref[...]

    b_all[:, yl, z] = b_half[yl]
    for other in range(8):
        filt_z[other, 0] = filt_t[other, z]
    tab_copy.wait()
    for j in range(3):
        tab_t[...] = tab_buf[j].T
        spec[pl.ds(32 * j, 32), 0:512] = tab_t[pl.ds(rows, 32), :].astype(F32)
    table = jnp.concatenate([spec[0:96, 0:256], spec[0:96, 256:512]], 0).astype(BF16)

    def tok_x(k):
        line = tok_all.at[pl.ds(xy * 8, 8)]
        return remote(line, line, tx_s.at[k], tx_r.at[k], xy_peer(k))

    for k in range(1, 8):
        tok_z(k).wait()
    for k in range(1, 8):
        tok_x(k).start()

    def filt_over_x(wave, k):
        spots = pl.ds(WAVES[wave], WAVES[wave + 1] - WAVES[wave])
        other = lax.rem(xy + k, 8)
        return remote(
            filt_z.at[other, spots], filt_x.at[xy, spots], fx_s.at[wave, k], fx_r.at[wave, k], xy_peer(k)
        )

    def ring(direction, step):
        which = lax.rem(z + (8 - step if direction > 0 else step), 8)
        chunk = b_all.at[:, :, which] if step < 3 else b_all.at[:, 0 if direction > 0 else 1, which]
        sems = (bp_s if direction > 0 else bm_s).at[step]
        return remote(chunk, chunk, sems, b_r.at[direction, step], z_peer(1 if direction > 0 else 7))

    def ring_on(step):
        for direction in (1, 0):
            ring(direction, step).wait()
            if step < 3:
                ring(direction, step + 1).start()

    swap.wait()
    ring(1, 0).start()
    ring(0, 0).start()

    for k in range(1, 8):
        tok_x(k).wait()

    def embed(chunk, carry):
        ids = jnp.concatenate([tok_all[chunk * 4 + i] for i in range(4)], 1)
        upper = ids >= 256
        hot = (lax.broadcasted_iota(jnp.int32, (256, 512), 0) == jnp.where(upper, ids - 256, ids))
        both = dot(table, hot.astype(F32).astype(BF16))
        value = jnp.where(upper, both[96:], both[:96])
        wide = jnp.concatenate([carry, value], 1)
        total = None
        parts = []
        for j in range(3):
            total = tin[:, j : j + 1] * value[32 * j : 32 * j + 32]
            for s in (1, 2):
                moved = pltpu.roll(wide[32 * j : 32 * j + 32], s, 1)[:, 128:]
                total = total + tin[:, 3 * s + j : 3 * s + j + 1] * moved
            parts.append(total)
        gate = (parts[1] * parts[2]).astype(BF16).astype(F32)
        for i in range(4):
            at = pl.ds(pl.multiple_of((chunk * 4 + i) * 32, 32), 32)
            gated[at, :] = gate[:, i * 128 : (i + 1) * 128]
            query[at, :] = parts[0][:, i * 128 : (i + 1) * 128]
        return value[:, 384:]

    def wave_on(wave):
        for k in NEAR[max(1, WAVES[wave]) : WAVES[wave + 1]]:
            filt_along_z(k).wait()
        for k in range(1, 8):
            filt_over_x(wave, k).start()

    carry = lax.fori_loop(0, 8, embed, jnp.zeros((96, 128), F32))
    wave_on(0)
    lax.fori_loop(8, 16, embed, carry)
    wave_on(1)
    wave_on(2)
    filt_x[xy] = filt_z[xy]

    def first():
        return dft_ref[0:128, :]

    def last():
        return jnp.concatenate([dft_ref[128:192, :], dft_ref[192:256, :]], 1)

    def inner():
        return jnp.concatenate([dft_ref[256:512, :], dft_ref[512:768, :]], 1)

    def turns():
        return turn_ref[0:64, :], turn_ref[64:128, :]

    def forward(source, group):
        columns = [source[pl.ds(group * 8 + i, 64, stride=32), :] for i in range(8)]
        column = jnp.concatenate(columns, 1).astype(BF16)
        stage = dot(first(), jnp.concatenate([column, column], 0))
        cos, sin = turns()
        turned_rows = []
        for i in range(8):
            re, im = stage[:64, i * 128 : (i + 1) * 128], stage[64:, i * 128 : (i + 1) * 128]
            turned_rows.append(jnp.concatenate([re * cos + im * sin, im * cos - re * sin], 1))
        return dot(jnp.concatenate(turned_rows, 0).astype(BF16), inner())

    def signal_side(group, _):
        spec[pl.ds(pl.multiple_of(group * 512, 512), 512), 0:256] = forward(gated, group)
        return 0

    lax.fori_loop(0, 4, signal_side, 0)
    for k in range(1, 8):
        filt_over_x(0, k).wait()
    ring_on(0)
    for wave in (1, 2):
        for k in range(1, 8):
            filt_over_x(wave, k).wait()
    for other in range(8):
        for spot in range(8):
            from_z = lax.rem(z + 8 - NEAR[spot], 8)
            at = pl.ds(pl.multiple_of((other * 8 + from_z) * 32, 32), 32)
            filt_f[at, :] = filt_x[other, spot].astype(F32)

    def filter_side(group, _):
        h = forward(filt_f, group)
        s = spec[pl.ds(pl.multiple_of(group * 512, 512), 512), 0:256]
        sr, si, hr, hi = s[:, :128], s[:, 128:], h[:, :128], h[:, 128:]
        product = jnp.concatenate([sr * hr - si * hi, sr * hi + si * hr], 1).astype(BF16)
        back = dot_t(product, inner())
        cos, sin = turns()
        parts = []
        for i in range(8):
            re, im = back[i * 64 : (i + 1) * 64, :128], back[i * 64 : (i + 1) * 64, 128:]
            parts.append(jnp.concatenate([re * cos - im * sin, im * cos + re * sin], 0))
        column = jnp.concatenate(parts, 1).astype(BF16)
        result = dot(last(), jnp.concatenate([column, column], 0)) * (1.0 / 8192)
        for i in range(8):
            long_f[pl.ds(group * 8 + i, 64, stride=32), :] = result[:, i * 128 : (i + 1) * 128]
        return 0

    lax.fori_loop(0, 4, filter_side, 0)

    skip = jnp.broadcast_to(tin[:, 9:10], (32, 128))
    for index in range(64):
        x_, yl_, z_ = index // 16, (index // 8) % 2, index % 8
        at = pl.ds(index * 32, 32)
        rounded = long_f[at, :].astype(BF16).astype(F32)
        value = (query[at, :] * (rounded + skip * gated[at, :])).astype(BF16)
        send_a[(x_ // 2) * 2 + yl_, x_ % 2, z_] = value

    order = [lax.rem(y + off, 4) for off in (2, 1, 3, 0)]

    def a_z(t, k):
        q = order[t]
        return remote(
            send_a.at[q, :, lax.rem(z + k, 8)], all_a.at[x, q, :, z], az_s.at[t, k], az_r.at[t, k], z_peer(k)
        )

    def a_x(t, right):
        mine = all_a.at[x, order[t]]
        return remote(mine, mine, ax_s.at[t, right], ax_r.at[t, right], x_peer(1 if right else 3))

    def a_on(t, right):
        half = all_a.at[lax.rem(x + (3 if right else 1), 4), order[t], right]
        return remote(half, half, ax_s.at[t, 2 + right], ax_r.at[t, 2 + right], x_peer(1 if right else 3))

    def pass_on(t):
        for right in (1, 0):
            a_x(t, right).wait()
            a_on(t, right).start()

    def start_a_z(t):
        for k in NEAR[1:]:
            a_z(t, k).start()
        all_a[x, order[t], :, z] = send_a[order[t], :, z]

    start_a_z(0)
    start_a_z(1)
    ring_on(1)
    start_a_z(2)

    def c_core(t):
        return remote(c_send.at[t], c_recv.at[t], cc_s.at[t], cc_r.at[t], core_peer)

    def c_y(t):
        return remote(y_send.at[t], y_recv.at[t], cy_s.at[t], cy_r.at[t], y_peer((2, 1, 3)[t]))

    def after_core(t):
        c_core(t).wait()
        total = c_mine[t] + c_recv[t].astype(F32)
        if t < 3:
            y_send[t] = total.astype(BF16)
            c_y(t).start()
        else:
            c_mine[t] = total

    def z_to_x(t):
        for k in NEAR[1:]:
            a_z(t, k).wait()
        for right in (1, 0):
            a_x(t, right).start()
        if t > 0:
            pass_on(t - 1)

    def multiply(t):
        for right in (1, 0):
            a_on(t, right).wait()

        def columns(part, _):
            at = pl.ds(pl.multiple_of(part * 256, 256), 256)
            total = None
            for xs in range(4):
                blocks = [all_a[xs, order[t], lo].reshape(256, 128) for lo in range(2)]
                weights = b_all[part].reshape(256, 1024)[:, xs * 256 : (xs + 1) * 256]
                term = dot(weights, jnp.concatenate(blocks, 1))
                total = term if total is None else total + term

            @pl.when(core == 0)
            def _():
                c_mine[t, at, :] = total[:, :128]
                c_send[t, at, :] = total[:, 128:].astype(BF16)

            @pl.when(core == 1)
            def _():
                c_mine[t, at, :] = total[:, 128:]
                c_send[t, at, :] = total[:, :128].astype(BF16)

            return 0

        lax.fori_loop(0, 3, columns, 0)
        c_core(t).start()

    z_to_x(0)
    z_to_x(1)
    ring_on(2)
    start_a_z(3)
    z_to_x(2)
    z_to_x(3)
    ring_on(3)
    multiply(0)
    multiply(1)
    after_core(0)
    pass_on(3)
    multiply(2)
    after_core(1)
    multiply(3)
    after_core(2)
    after_core(3)
    for t in range(3):
        c_y(t).wait()
    summed = c_mine[3] + y_recv[0].astype(F32) + y_recv[1].astype(F32) + y_recv[2].astype(F32)
    projected = jnp.concatenate([summed[i * 128 : (i + 1) * 128].T for i in range(6)], 1).astype(BF16)

    halo = remote(halo_send, halo_recv, h_s, h_r, owner(place + 1))
    halo_send[...] = projected[112:]
    pl.when(has_next)(lambda: halo.start())

    @pl.when(place == 0)
    def _():
        halo_recv[...] = jnp.zeros_like(halo_recv)

    pl.when(has_next)(lambda: halo.wait_send())
    pl.when(has_prev)(lambda: halo.wait_recv())
    pl.when(is_turned)(lambda: taps_copy.wait())
    wide = jnp.concatenate([halo_recv[...], projected], 0).astype(F32)

    def shifted(value, s):
        return value if s == 0 else pltpu.roll(value, s, 0)

    feats = []
    for j in range(3):
        part = wide[:, j * 256 : (j + 1) * 256]
        total = None
        for s in range(3):
            term = taps_mine[3 * s + j : 3 * s + j + 1, :] * shifted(part, s)
            total = term if total is None else total + term
        feats.append(total)
    gate = feats[1] * feats[2]
    short = None
    for s in range(7):
        term = taps_mine[9 + s : 10 + s, :] * shifted(gate, s)
        short = term if short is None else short + term
    mixed = (feats[0] * (short + taps_mine[16:17, :] * gate))[16:].astype(BF16)

    out_send[...] = mixed
    out_copy = remote(out_send, out_recv, o_s, o_r, turned)

    @pl.when(is_turned)
    def _():
        out_copy.start()
        out_copy.wait()

    @pl.when(x == ch)
    def _():
        out_recv[...] = out_send[...]

    out_ref[...] = out_recv[...]


def per_device(token_ids, tables, filter_long, skip_long, taps_in, projection, taps_proj, taps_short, skip_short):
    vmem = pl.BlockSpec(memory_space=pltpu.VMEM)
    hbm = pl.BlockSpec(memory_space=pltpu.HBM)
    tables_dft = [jnp.asarray(t) for t in dft_tables()]
    dma = pltpu.SemaphoreType.DMA
    scratch = [
        pltpu.VMEM((1, 128), jnp.int32),
        pltpu.VMEM((128, 2048), BF16),
        pltpu.VMEM((3, 3, 2048), F32),
        pltpu.VMEM((16, 128), F32),
        pltpu.VMEM((3, 16, 2048), BF16),
        pltpu.VMEM((3, 3, 256), F32),
        pltpu.VMEM((7, 256), F32),
        pltpu.VMEM((2, 128), F32),
        *[pltpu.VMEM(t.shape, t.dtype) for t in tables_dft],
        pltpu.VMEM((24, 256), F32),
        dma((10,)),
        pltpu.VMEM((64, 1, 128), jnp.int32),
        pltpu.VMEM((3, 512, 128), BF16),
        pltpu.VMEM((128, 512), BF16),
        pltpu.VMEM((128, 16), F32),
        pltpu.VMEM((8, 8, 32, 128), BF16),
        pltpu.VMEM((8, 8, 32, 128), BF16),
        pltpu.VMEM((8, 8, 32, 128), BF16),
        pltpu.VMEM((2048, 128), F32),
        pltpu.VMEM((2048, 128), F32),
        pltpu.VMEM((2048, 128), F32),
        pltpu.VMEM((2048, 128), F32),
        pltpu.VMEM((2048, 512), F32),
        pltpu.VMEM((4, 2, 8, 32, 128), BF16),
        pltpu.VMEM((4, 4, 2, 8, 32, 128), BF16),
        pltpu.VMEM((2, 3, 16, 1024), BF16),
        pltpu.VMEM((3, 2, 8, 16, 1024), BF16),
        pltpu.VMEM((4, 768, 128), BF16),
        pltpu.VMEM((4, 768, 128), BF16),
        pltpu.VMEM((4, 768, 128), F32),
        pltpu.VMEM((3, 768, 128), BF16),
        pltpu.VMEM((3, 768, 128), BF16),
        pltpu.VMEM((24, 256), F32),
        pltpu.VMEM((16, 768), BF16),
        pltpu.VMEM((16, 768), BF16),
        pltpu.VMEM((128, 256), BF16),
        pltpu.VMEM((128, 256), BF16),
        dma, dma((8,)), dma((8,)), dma((8,)), dma((8,)),
        dma((8,)), dma((8,)), dma((3, 8)), dma((3, 8)),
        dma, dma, dma((4,)), dma((4,)), dma((2, 4)),
        dma((4, 8)), dma((4, 8)), dma((4, 4)), dma((4, 4)),
        dma((4,)), dma((4,)), dma((3,)), dma((3,)),
        dma, dma, dma, dma, dma, dma,
    ]
    return pl.pallas_call(
        kernel,
        out_shape=jax.ShapeDtypeStruct((128, 256), BF16),
        in_specs=[hbm] * 11,
        out_specs=vmem,
        scratch_shapes=scratch,
        compiler_params=pltpu.CompilerParams(
            collective_id=0, has_side_effects=True, vmem_limit_bytes=60 * 2**20
        ),
    )(
        token_ids.reshape(1, 128), jnp.transpose(tables, (1, 0, 2)), filter_long, taps_in,
        skip_long.reshape(16, 128), jnp.transpose(projection, (1, 2, 0)), taps_proj, taps_short,
        skip_short.reshape(2, 128), *tables_dft,
    )


def solution(mesh):
    placed = (
        P("ctx"),
        P(None, None, "ch"),
        P("ctx", "ch"),
        P("ch"),
        P(None, None, "ch"),
        P("ch", None, "ctx"),
        P(None, None, "ch"),
        P(None, "ch"),
        P("ch"),
    )
    return jax.shard_map(
        per_device, mesh=mesh, in_specs=placed, out_specs=P("ctx", "ch"), check_vma=False
    )
```

```python
import functools

import jax
import jax.numpy as jnp
import numpy as np
from jax import lax
from jax.experimental import pallas as pl
from jax.experimental.pallas import tpu as pltpu
from jax.sharding import PartitionSpec as P

MESH = pl.DeviceIdType.MESH
F32, BF16 = jnp.float32, jnp.bfloat16
NEAR = (0, 1, 7, 2, 6, 3, 5, 4)
WAVES = (0, 5, 7, 8)
SPOT = tuple(NEAR.index(k) for k in range(8))


def dft_tables():
    k1 = np.arange(64)[:, None] + 0.25
    phase = 2 * np.pi * k1 * np.arange(64)[None, :] / 64
    rows = np.concatenate([np.cos(phase), -np.sin(phase)], 0)

    def split(table):
        high = table.astype(BF16)
        return high, (table - high.astype(np.float64)).astype(BF16)

    high, low = split(rows)
    first = np.concatenate([high, low], 1)
    turn = 2 * np.pi * k1 * np.arange(128)[None, :] / 8192
    inner = 2 * np.pi * np.outer(np.arange(128), np.arange(128)) / 128
    cos, sin = np.cos(inner), np.sin(inner)
    both = np.concatenate([np.concatenate([cos, -sin], 1), np.concatenate([sin, cos], 1)], 0)
    w_high = both.astype(BF16)
    tall = [first, high.T, low.T, *np.split(w_high, 2, 1)]
    return np.concatenate(tall, 0), np.concatenate([np.cos(turn), np.sin(turn)], 0).astype(np.float32)


def dot(left, right):
    return jnp.dot(left, right, preferred_element_type=F32)


def dot_t(left, right):
    return lax.dot_general(left, right, (((1,), (1,)), ((), ())), preferred_element_type=F32)


def kernel(
    tok_hbm, tab_hbm, filt_hbm, tin_hbm, skip_hbm, proj_hbm, tpr_hbm, tsh_hbm, ssk_hbm,
    dft_hbm, turn_hbm,
    out_ref,
    tok_ref, filt_ref, tin_ref, skip_ref, proj_ref, tpr_ref, tsh_ref, ssk_ref,
    dft_ref, turn_ref, tout_ref, load_sem,
    tok_all, tab_buf, tab_t, tin_t, filt_t, filt_z, filt_x, filt_f, gated, query, long_f,
    spec, send_a, all_a, b_half, b_all, c_send, c_recv, c_mine, y_send, y_recv,
    taps_mine, halo_send, halo_recv, out_send, out_recv,
    tab_sem, tz_s, tz_r, tx_s, tx_r, fz_s, fz_r, fx_s, fx_r, sw_s, sw_r, bp_s, bm_s, b_r,
    az_s, az_r, ax_s, ax_r, cc_s, cc_r, cy_s, cy_r, tp_s, tp_r, h_s, h_r, o_s, o_r,
    lz_s, lz_r, lx_s, lx_r,
):
    ctx, ch = lax.axis_index("ctx"), lax.axis_index("ch")
    x, yl, z = ctx // 16, (ctx // 8) % 2, ctx % 8
    yh, core = ch // 2, ch % 2
    xy = x * 2 + yl
    y = yh * 2 + yl

    def dev(x_, yl_, z_, ch_):
        return {"ctx": x_ * 16 + yl_ * 8 + z_, "ch": ch_}

    def z_peer(k):
        return dev(x, yl, lax.rem(z + k, 8), ch)

    def xy_peer(k):
        other = lax.rem(xy + k, 8)
        return dev(other // 2, other % 2, z, ch)

    def x_peer(k):
        return dev(lax.rem(x + k, 4), yl, z, ch)

    core_peer = dev(x, yl, z, yh * 2 + 1 - core)

    def y_peer(k):
        other = lax.rem(y + k, 4)
        return dev(x, other % 2, z, (other // 2) * 2 + core)

    turned = dev(ch, yl, z, x)
    is_turned = x != ch
    place = ch * 16 + yl * 8 + z

    def owner(index):
        return dev(x, (index // 8) % 2, index % 8, index // 16)

    has_next, has_prev = place < 63, place > 0

    def remote(src, dst, send, recv, device):
        return pltpu.make_async_remote_copy(
            src_ref=src, dst_ref=dst, send_sem=send, recv_sem=recv, device_id=device, device_id_type=MESH
        )

    lanes = pl.multiple_of((ctx // 4) * 128, 128)
    tab_copy = pltpu.make_async_copy(tab_hbm.at[:, :, pl.ds(lanes, 128)], tab_buf, tab_sem)
    pairs = (
        (filt_hbm, filt_ref), (tok_hbm, tok_ref), (proj_hbm, proj_ref), (tin_hbm, tin_ref),
        (skip_hbm, skip_ref), (tpr_hbm, tpr_ref), (tsh_hbm, tsh_ref), (ssk_hbm, ssk_ref),
        (dft_hbm, dft_ref), (turn_hbm, turn_ref),
    )
    loads = [pltpu.make_async_copy(src, dst, load_sem.at[i]) for i, (src, dst) in enumerate(pairs)]
    for load in loads:
        load.start()
    tab_copy.start()

    bar = pltpu.get_barrier_semaphore()

    def greet(device):
        pl.semaphore_signal(bar, inc=1, device_id=device, device_id_type=MESH)

    for k in range(1, 8):
        greet(z_peer(k))
        greet(xy_peer(k))
    greet(dev(x, yl, z, (1 - yh) * 2 + core))
    greet(dev(x, 1 - yl, z, (1 - yh) * 2 + core))
    greet(core_peer)
    pl.when(is_turned)(lambda: greet(turned))
    pl.when((z == 7) & has_next)(lambda: greet(owner(place + 1)))
    pl.when((z == 0) & has_prev)(lambda: greet(owner(place - 1)))

    loads[0].wait()
    for group in range(16):
        block = filt_ref[:, group * 128 : (group + 1) * 128].T
        for part in range(4):
            index = group * 4 + part
            filt_t[index // 8, index % 8] = block[part * 32 : (part + 1) * 32]
    loads[1].wait()
    tok_all[ctx] = tok_ref[...]
    expected = 17 + jnp.where(is_turned, 1, 0)
    expected += jnp.where((z == 7) & has_next, 1, 0) + jnp.where((z == 0) & has_prev, 1, 0)
    pl.semaphore_wait(bar, expected)

    def tok_z(k):
        return remote(tok_all.at[ctx], tok_all.at[ctx], tz_s.at[k], tz_r.at[k], z_peer(k))

    def filt_along_z(k):
        return remote(
            filt_t.at[:, lax.rem(z + k, 8)], filt_z.at[:, SPOT[k]], fz_s.at[k], fz_r.at[k], z_peer(k)
        )

    for k in range(1, 8):
        tok_z(k).start()
    for k in NEAR[1:]:
        filt_along_z(k).start()
    for load in loads[2:]:
        load.wait()
    for half in range(2):
        for part in range(4):
            start = part * 512 + half * 256
            b_half[half, :, :, part * 256 : (part + 1) * 256] = proj_ref[:, :, start : start + 256]
    stacked = [tin_ref[s, :, pl.ds(lanes, 128)] for s in range(3)] + [skip_ref[pl.ds(ctx // 4, 1), :]]
    tin_t[...] = jnp.concatenate(stacked + [jnp.zeros((6, 128), F32)], 0).T
    for s in range(3):
        tout_ref[3 * s : 3 * s + 3, :] = tpr_ref[s]
    tout_ref[9:16, :] = tsh_ref[...]
    tout_ref[16:17, :] = jnp.concatenate([ssk_ref[0:1, :], ssk_ref[1:2, :]], 1)
    tout_ref[17:24, :] = jnp.zeros((7, 256), F32)
    rows = pl.multiple_of((ctx % 4) * 32, 32)
    tin = tin_t[pl.ds(rows, 32), :]

    swap = remote(b_half.at[1 - yl], b_all.at[:, yl, z], sw_s, sw_r, dev(x, 1 - yl, z, ch))
    swap.start()
    taps_copy = remote(tout_ref, taps_mine, tp_s, tp_r, turned)
    pl.when(is_turned)(lambda: taps_copy.start())

    @pl.when(x == ch)
    def _():
        taps_mine[...] = tout_ref[...]

    b_all[:, yl, z] = b_half[yl]
    for other in range(8):
        filt_z[other, 0] = filt_t[other, z]
    tab_copy.wait()
    for j in range(3):
        tab_t[...] = tab_buf[j].T
        spec[pl.ds(32 * j, 32), 0:512] = tab_t[pl.ds(rows, 32), :].astype(F32)
    table = jnp.concatenate([spec[0:96, 0:256], spec[0:96, 256:512]], 0).astype(BF16)

    def tok_x(k):
        line = tok_all.at[pl.ds(xy * 8, 8)]
        return remote(line, line, tx_s.at[k], tx_r.at[k], xy_peer(k))

    for k in range(1, 8):
        tok_z(k).wait()
    for k in range(1, 8):
        tok_x(k).start()

    def filt_over_x(wave, k):
        spots = pl.ds(WAVES[wave], WAVES[wave + 1] - WAVES[wave])
        other = lax.rem(xy + k, 8)
        return remote(
            filt_z.at[other, spots], filt_x.at[xy, spots], fx_s.at[wave, k], fx_r.at[wave, k], xy_peer(k)
        )

    def ring(direction, step):
        which = lax.rem(z + (8 - step if direction > 0 else step), 8)
        chunk = b_all.at[:, :, which] if step < 3 else b_all.at[:, 0 if direction > 0 else 1, which]
        sems = (bp_s if direction > 0 else bm_s).at[step]
        return remote(chunk, chunk, sems, b_r.at[direction, step], z_peer(1 if direction > 0 else 7))

    def ring_on(step):
        for direction in (1, 0):
            ring(direction, step).wait()
            if step < 3:
                ring(direction, step + 1).start()

    swap.wait()
    ring(1, 0).start()
    ring(0, 0).start()

    for k in range(1, 8):
        tok_x(k).wait()

    def embed(chunk, carry):
        ids = jnp.concatenate([tok_all[chunk * 4 + i] for i in range(4)], 1)
        upper = ids >= 256
        hot = (lax.broadcasted_iota(jnp.int32, (256, 512), 0) == jnp.where(upper, ids - 256, ids))
        both = dot(table, hot.astype(F32).astype(BF16))
        value = jnp.where(upper, both[96:], both[:96])
        wide = jnp.concatenate([carry, value], 1)
        total = None
        parts = []
        for j in range(3):
            total = tin[:, j : j + 1] * value[32 * j : 32 * j + 32]
            for s in (1, 2):
                moved = pltpu.roll(wide[32 * j : 32 * j + 32], s, 1)[:, 128:]
                total = total + tin[:, 3 * s + j : 3 * s + j + 1] * moved
            parts.append(total)
        gate = (parts[1] * parts[2]).astype(BF16).astype(F32)
        for i in range(4):
            at = pl.ds(pl.multiple_of((chunk * 4 + i) * 32, 32), 32)
            gated[at, :] = gate[:, i * 128 : (i + 1) * 128]
            query[at, :] = parts[0][:, i * 128 : (i + 1) * 128]
        return value[:, 384:]

    def wave_on(wave):
        for k in NEAR[max(1, WAVES[wave]) : WAVES[wave + 1]]:
            filt_along_z(k).wait()
        for k in range(1, 8):
            filt_over_x(wave, k).start()

    carry = lax.fori_loop(0, 8, embed, jnp.zeros((96, 128), F32))
    wave_on(0)
    lax.fori_loop(8, 16, embed, carry)
    wave_on(1)
    wave_on(2)
    filt_x[xy] = filt_z[xy]

    def first():
        return dft_ref[0:128, :]

    def last():
        return jnp.concatenate([dft_ref[128:192, :], dft_ref[192:256, :]], 1)

    def inner():
        return jnp.concatenate([dft_ref[256:512, :], dft_ref[512:768, :]], 1)

    def turns():
        return turn_ref[0:64, :], turn_ref[64:128, :]

    def forward(source, group):
        columns = [source[pl.ds(group * 8 + i, 64, stride=32), :] for i in range(8)]
        column = jnp.concatenate(columns, 1).astype(BF16)
        stage = dot(first(), jnp.concatenate([column, column], 0))
        cos, sin = turns()
        turned_rows = []
        for i in range(8):
            re, im = stage[:64, i * 128 : (i + 1) * 128], stage[64:, i * 128 : (i + 1) * 128]
            turned_rows.append(jnp.concatenate([re * cos + im * sin, im * cos - re * sin], 1))
        return dot(jnp.concatenate(turned_rows, 0).astype(BF16), inner())

    def signal_side(group, _):
        spec[pl.ds(pl.multiple_of(group * 512, 512), 512), 0:256] = forward(gated, group)
        return 0

    lax.fori_loop(0, 4, signal_side, 0)
    for k in range(1, 8):
        filt_over_x(0, k).wait()
    ring_on(0)
    for wave in (1, 2):
        for k in range(1, 8):
            filt_over_x(wave, k).wait()
    for other in range(8):
        for spot in range(8):
            from_z = lax.rem(z + 8 - NEAR[spot], 8)
            at = pl.ds(pl.multiple_of((other * 8 + from_z) * 32, 32), 32)
            filt_f[at, :] = filt_x[other, spot].astype(F32)

    def filter_side(group, _):
        h = forward(filt_f, group)
        s = spec[pl.ds(pl.multiple_of(group * 512, 512), 512), 0:256]
        sr, si, hr, hi = s[:, :128], s[:, 128:], h[:, :128], h[:, 128:]
        product = jnp.concatenate([sr * hr - si * hi, sr * hi + si * hr], 1).astype(BF16)
        back = dot_t(product, inner())
        cos, sin = turns()
        parts = []
        for i in range(8):
            re, im = back[i * 64 : (i + 1) * 64, :128], back[i * 64 : (i + 1) * 64, 128:]
            parts.append(jnp.concatenate([re * cos - im * sin, im * cos + re * sin], 0))
        column = jnp.concatenate(parts, 1).astype(BF16)
        result = dot(last(), jnp.concatenate([column, column], 0)) * (1.0 / 8192)
        for i in range(8):
            long_f[pl.ds(group * 8 + i, 64, stride=32), :] = result[:, i * 128 : (i + 1) * 128]
        return 0

    lax.fori_loop(0, 4, filter_side, 0)

    skip = jnp.broadcast_to(tin[:, 9:10], (32, 128))
    for index in range(64):
        x_, yl_, z_ = index // 16, (index // 8) % 2, index % 8
        at = pl.ds(index * 32, 32)
        rounded = long_f[at, :].astype(BF16).astype(F32)
        value = (query[at, :] * (rounded + skip * gated[at, :])).astype(BF16)
        send_a[(x_ // 2) * 2 + yl_, x_ % 2, z_] = value

    order = [lax.rem(y + off, 4) for off in (2, 1, 3, 0)]

    def a_z(t, k):
        q = order[t]
        return remote(
            send_a.at[q, :, lax.rem(z + k, 8)], all_a.at[x, q, :, z], az_s.at[t, k], az_r.at[t, k], z_peer(k)
        )

    def a_x(t, right):
        mine = all_a.at[x, order[t]]
        return remote(mine, mine, ax_s.at[t, right], ax_r.at[t, right], x_peer(1 if right else 3))

    def a_on(t, right):
        half = all_a.at[lax.rem(x + (3 if right else 1), 4), order[t], right]
        return remote(half, half, ax_s.at[t, 2 + right], ax_r.at[t, 2 + right], x_peer(1 if right else 3))

    def pass_on(t):
        for right in (1, 0):
            a_x(t, right).wait()
            a_on(t, right).start()

    def start_a_z(t):
        for k in NEAR[1:]:
            a_z(t, k).start()
        all_a[x, order[t], :, z] = send_a[order[t], :, z]

    def last_block(part):
        return 1 - core if part == 0 else core

    def last_z(part, k):
        return remote(
            send_a.at[order[3], last_block(part), lax.rem(z + k, 8)],
            all_a.at[x, order[3], last_block(part), z],
            lz_s.at[part, k], lz_r.at[part, k], z_peer(k),
        )

    def last_x(part, k):
        mine = all_a.at[x, order[3], last_block(part)]
        return remote(mine, mine, lx_s.at[part, k], lx_r.at[part, k], x_peer(k))

    def start_last_z(part):
        for k in NEAR[1:]:
            last_z(part, k).start()
        all_a[x, order[3], last_block(part), z] = send_a[order[3], last_block(part), z]

    def last_z_to_x(part):
        for k in NEAR[1:]:
            last_z(part, k).wait()
        for k in (1, 3, 2):
            last_x(part, k).start()

    def last_multiply(part):
        for k in (1, 3, 2):
            last_x(part, k).wait()
        block = jnp.concatenate([all_a[xs, order[3], last_block(part)].reshape(256, 128) for xs in range(4)], 0)
        return dot(b_all[...].reshape(768, 1024), block)

    start_a_z(0)
    start_a_z(1)
    ring_on(1)
    start_a_z(2)

    def c_core(t):
        return remote(c_send.at[t], c_recv.at[t], cc_s.at[t], cc_r.at[t], core_peer)

    def c_y(t):
        return remote(y_send.at[t], y_recv.at[t], cy_s.at[t], cy_r.at[t], y_peer((2, 1, 3)[t]))

    def after_core(t):
        c_core(t).wait()
        total = c_mine[t] + c_recv[t].astype(F32)
        y_send[t] = total.astype(BF16)
        c_y(t).start()

    def z_to_x(t):
        for k in NEAR[1:]:
            a_z(t, k).wait()
        for right in (1, 0):
            a_x(t, right).start()

    def multiply(t):
        for right in (1, 0):
            a_on(t, right).wait()

        total = None
        for xs in range(4):
            blocks = [all_a[xs, order[t], lo].reshape(256, 128) for lo in range(2)]
            weights = b_all[...].reshape(768, 1024)[:, xs * 256 : (xs + 1) * 256]
            term = dot(weights, jnp.concatenate(blocks, 1))
            total = term if total is None else total + term

        @pl.when(core == 0)
        def _():
            c_mine[t] = total[:, :128]
            c_send[t] = total[:, 128:].astype(BF16)

        @pl.when(core == 1)
        def _():
            c_mine[t] = total[:, 128:]
            c_send[t] = total[:, :128].astype(BF16)

        c_core(t).start()

    z_to_x(0)
    z_to_x(1)
    pass_on(0)
    ring_on(2)
    start_last_z(0)
    start_last_z(1)
    z_to_x(2)
    pass_on(1)
    ring_on(3)
    multiply(0)
    pass_on(2)
    multiply(1)
    after_core(0)
    last_z_to_x(0)
    after_core(1)
    last_z_to_x(1)
    multiply(2)
    c_send[3] = last_multiply(0).astype(BF16)
    c_core(3).start()
    after_core(2)
    summed = last_multiply(1)
    c_core(3).wait()
    summed += c_recv[3].astype(F32)
    for t in range(3):
        c_y(t).wait()
        summed += y_recv[t].astype(F32)
    projected = jnp.concatenate([summed[i * 128 : (i + 1) * 128].T for i in range(6)], 1).astype(BF16)

    halo = remote(halo_send, halo_recv, h_s, h_r, owner(place + 1))
    halo_send[...] = projected[112:]
    pl.when(has_next)(lambda: halo.start())

    pl.when(is_turned)(lambda: taps_copy.wait())

    def shifted(value, s):
        return value if s == 0 else pltpu.roll(value, s, 0)

    def mix(wide):
        feats = []
        for j in range(3):
            part = wide[:, j * 256 : (j + 1) * 256].astype(F32)
            total = None
            for s in range(3):
                term = taps_mine[3 * s + j : 3 * s + j + 1, :] * shifted(part, s)
                total = term if total is None else total + term
            feats.append(total)
        gate = feats[1] * feats[2]
        short = None
        for s in range(7):
            term = taps_mine[9 + s : 10 + s, :] * shifted(gate, s)
            short = term if short is None else short + term
        return (feats[0] * (short + taps_mine[16:17, :] * gate))[16:].astype(BF16)

    def out_copy(part):
        at = (pl.ds(16, 112), pl.ds(0, 16))[part]
        return remote(out_send.at[at], out_recv.at[at], o_s.at[part], o_r.at[part], turned)

    out_send[16:] = mix(projected)
    pl.when(is_turned)(lambda: out_copy(0).start())

    @pl.when(place == 0)
    def _():
        halo_recv[...] = jnp.zeros_like(halo_recv)

    pl.when(has_next)(lambda: halo.wait_send())
    pl.when(has_prev)(lambda: halo.wait_recv())
    out_send[0:16] = mix(jnp.concatenate([halo_recv[...], projected[:16]], 0))

    @pl.when(is_turned)
    def _():
        out_copy(1).start()
        out_copy(0).wait()
        out_copy(1).wait()

    @pl.when(x == ch)
    def _():
        out_recv[...] = out_send[...]

    out_ref[...] = out_recv[...]


def per_device(token_ids, tables, filter_long, skip_long, taps_in, projection, taps_proj, taps_short, skip_short):
    vmem = pl.BlockSpec(memory_space=pltpu.VMEM)
    hbm = pl.BlockSpec(memory_space=pltpu.HBM)
    tables_dft = [jnp.asarray(t) for t in dft_tables()]
    dma = pltpu.SemaphoreType.DMA
    scratch = [
        pltpu.VMEM((1, 128), jnp.int32),
        pltpu.VMEM((128, 2048), BF16),
        pltpu.VMEM((3, 3, 2048), F32),
        pltpu.VMEM((16, 128), F32),
        pltpu.VMEM((3, 16, 2048), BF16),
        pltpu.VMEM((3, 3, 256), F32),
        pltpu.VMEM((7, 256), F32),
        pltpu.VMEM((2, 128), F32),
        *[pltpu.VMEM(t.shape, t.dtype) for t in tables_dft],
        pltpu.VMEM((24, 256), F32),
        dma((10,)),
        pltpu.VMEM((64, 1, 128), jnp.int32),
        pltpu.VMEM((3, 512, 128), BF16),
        pltpu.VMEM((128, 512), BF16),
        pltpu.VMEM((128, 16), F32),
        pltpu.VMEM((8, 8, 32, 128), BF16),
        pltpu.VMEM((8, 8, 32, 128), BF16),
        pltpu.VMEM((8, 8, 32, 128), BF16),
        pltpu.VMEM((2048, 128), F32),
        pltpu.VMEM((2048, 128), F32),
        pltpu.VMEM((2048, 128), F32),
        pltpu.VMEM((2048, 128), F32),
        pltpu.VMEM((2048, 512), F32),
        pltpu.VMEM((4, 2, 8, 32, 128), BF16),
        pltpu.VMEM((4, 4, 2, 8, 32, 128), BF16),
        pltpu.VMEM((2, 3, 16, 1024), BF16),
        pltpu.VMEM((3, 2, 8, 16, 1024), BF16),
        pltpu.VMEM((4, 768, 128), BF16),
        pltpu.VMEM((4, 768, 128), BF16),
        pltpu.VMEM((4, 768, 128), F32),
        pltpu.VMEM((3, 768, 128), BF16),
        pltpu.VMEM((3, 768, 128), BF16),
        pltpu.VMEM((24, 256), F32),
        pltpu.VMEM((16, 768), BF16),
        pltpu.VMEM((16, 768), BF16),
        pltpu.VMEM((128, 256), BF16),
        pltpu.VMEM((128, 256), BF16),
        dma, dma((8,)), dma((8,)), dma((8,)), dma((8,)),
        dma((8,)), dma((8,)), dma((3, 8)), dma((3, 8)),
        dma, dma, dma((4,)), dma((4,)), dma((2, 4)),
        dma((3, 8)), dma((3, 8)), dma((3, 4)), dma((3, 4)),
        dma((4,)), dma((4,)), dma((3,)), dma((3,)),
        dma, dma, dma, dma, dma((2,)), dma((2,)),
        dma((2, 8)), dma((2, 8)), dma((2, 4)), dma((2, 4)),
    ]
    return pl.pallas_call(
        kernel,
        out_shape=jax.ShapeDtypeStruct((128, 256), BF16),
        in_specs=[hbm] * 11,
        out_specs=vmem,
        scratch_shapes=scratch,
        compiler_params=pltpu.CompilerParams(
            collective_id=0, has_side_effects=True, vmem_limit_bytes=60 * 2**20
        ),
    )(
        token_ids.reshape(1, 128), jnp.transpose(tables, (1, 0, 2)), filter_long, taps_in,
        skip_long.reshape(16, 128), jnp.transpose(projection, (1, 2, 0)), taps_proj, taps_short,
        skip_short.reshape(2, 128), *tables_dft,
    )


def solution(mesh):
    placed = (
        P("ctx"),
        P(None, None, "ch"),
        P("ctx", "ch"),
        P("ch"),
        P(None, None, "ch"),
        P("ch", None, "ctx"),
        P(None, None, "ch"),
        P(None, "ch"),
        P("ch"),
    )
    return jax.shard_map(
        per_device, mesh=mesh, in_specs=placed, out_specs=P("ctx", "ch"), check_vma=False
    )
```

```python
import functools

import jax
import jax.numpy as jnp
import numpy as np
from jax import lax
from jax.experimental import pallas as pl
from jax.experimental.pallas import tpu as pltpu
from jax.sharding import PartitionSpec as P

MESH = pl.DeviceIdType.MESH
F32, BF16 = jnp.float32, jnp.bfloat16
NEAR = (0, 1, 7, 2, 6, 3, 5, 4)
WAVES = (0, 5, 7, 8)
SPOT = tuple(NEAR.index(k) for k in range(8))


def dft_tables():
    k1 = np.arange(64)[:, None] + 0.25
    phase = 2 * np.pi * k1 * np.arange(64)[None, :] / 64
    rows = np.concatenate([np.cos(phase), -np.sin(phase)], 0)

    def split(table):
        high = table.astype(BF16)
        return high, (table - high.astype(np.float64)).astype(BF16)

    high, low = split(rows)
    first = np.concatenate([high, low], 1)
    turn = 2 * np.pi * k1 * np.arange(128)[None, :] / 8192
    inner = 2 * np.pi * np.outer(np.arange(128), np.arange(128)) / 128
    cos, sin = np.cos(inner), np.sin(inner)
    both = np.concatenate([np.concatenate([cos, -sin], 1), np.concatenate([sin, cos], 1)], 0)
    w_high = both.astype(BF16)
    tall = [first, high.T, low.T, *np.split(w_high, 2, 1)]
    return np.concatenate(tall, 0), np.concatenate([np.cos(turn), np.sin(turn)], 0).astype(np.float32)


def dot(left, right):
    return jnp.dot(left, right, preferred_element_type=F32)


def dot_t(left, right):
    return lax.dot_general(left, right, (((1,), (1,)), ((), ())), preferred_element_type=F32)


def kernel(
    tok_hbm, tab_hbm, filt_hbm, tin_hbm, skip_hbm, proj_hbm, tpr_hbm, tsh_hbm, ssk_hbm,
    dft_hbm, turn_hbm,
    out_ref,
    tok_ref, filt_ref, tin_ref, skip_ref, proj_ref, tpr_ref, tsh_ref, ssk_ref,
    dft_ref, turn_ref, tout_ref, load_sem,
    tok_all, tab_buf, tab_t, tin_t, filt_t, filt_z, filt_x, filt_f, gated, query, long_f,
    spec, send_a, all_a, b_half, b_all, c_send, c_recv, c_mine, y_send, y_recv,
    taps_mine, halo_send, halo_recv, out_send, out_recv,
    tab_sem, tz_s, tz_r, tx_s, tx_r, fz_s, fz_r, fx_s, fx_r, sw_s, sw_r, bp_s, bm_s, b_r,
    az_s, az_r, ax_s, ax_r, cc_s, cc_r, cy_s, cy_r, tp_s, tp_r, h_s, h_r, o_s, o_r,
    lz_s, lz_r, lx_s, lx_r,
):
    ctx, ch = lax.axis_index("ctx"), lax.axis_index("ch")
    x, yl, z = ctx // 16, (ctx // 8) % 2, ctx % 8
    yh, core = ch // 2, ch % 2
    xy = x * 2 + yl
    y = yh * 2 + yl

    def dev(x_, yl_, z_, ch_):
        return {"ctx": x_ * 16 + yl_ * 8 + z_, "ch": ch_}

    def z_peer(k):
        return dev(x, yl, lax.rem(z + k, 8), ch)

    def xy_peer(k):
        other = lax.rem(xy + k, 8)
        return dev(other // 2, other % 2, z, ch)

    def x_peer(k):
        return dev(lax.rem(x + k, 4), yl, z, ch)

    core_peer = dev(x, yl, z, yh * 2 + 1 - core)

    def y_peer(k):
        other = lax.rem(y + k, 4)
        return dev(x, other % 2, z, (other // 2) * 2 + core)

    turned = dev(ch, yl, z, x)
    is_turned = x != ch
    place = ch * 16 + yl * 8 + z

    def owner(index):
        return dev(x, (index // 8) % 2, index % 8, index // 16)

    has_next, has_prev = place < 63, place > 0

    def remote(src, dst, send, recv, device):
        return pltpu.make_async_remote_copy(
            src_ref=src, dst_ref=dst, send_sem=send, recv_sem=recv, device_id=device, device_id_type=MESH
        )

    lanes = pl.multiple_of((ctx // 4) * 128, 128)
    tab_copy = pltpu.make_async_copy(tab_hbm.at[:, :, pl.ds(lanes, 128)], tab_buf, tab_sem)
    pairs = (
        (filt_hbm, filt_ref), (tok_hbm, tok_ref), (proj_hbm, proj_ref), (tin_hbm, tin_ref),
        (skip_hbm, skip_ref), (tpr_hbm, tpr_ref), (tsh_hbm, tsh_ref), (ssk_hbm, ssk_ref),
        (dft_hbm, dft_ref), (turn_hbm, turn_ref),
    )
    loads = [pltpu.make_async_copy(src, dst, load_sem.at[i]) for i, (src, dst) in enumerate(pairs)]
    loads[0].start()

    bar = pltpu.get_barrier_semaphore()

    def greet(device):
        pl.semaphore_signal(bar, inc=1, device_id=device, device_id_type=MESH)

    for k in range(1, 8):
        greet(z_peer(k))
        greet(xy_peer(k))
    greet(dev(x, yl, z, (1 - yh) * 2 + core))
    greet(dev(x, 1 - yl, z, (1 - yh) * 2 + core))
    greet(core_peer)
    pl.when(is_turned)(lambda: greet(turned))
    pl.when((z == 7) & has_next)(lambda: greet(owner(place + 1)))
    pl.when((z == 0) & has_prev)(lambda: greet(owner(place - 1)))

    for load in loads[1:]:
        load.start()
    tab_copy.start()
    loads[0].wait()
    for group in range(16):
        block = filt_ref[:, group * 128 : (group + 1) * 128].T
        for part in range(4):
            index = group * 4 + part
            filt_t[index // 8, index % 8] = block[part * 32 : (part + 1) * 32]
    loads[1].wait()
    tok_all[ctx] = tok_ref[...]
    expected = 17 + jnp.where(is_turned, 1, 0)
    expected += jnp.where((z == 7) & has_next, 1, 0) + jnp.where((z == 0) & has_prev, 1, 0)
    pl.semaphore_wait(bar, expected)

    def tok_z(k):
        return remote(tok_all.at[ctx], tok_all.at[ctx], tz_s.at[k], tz_r.at[k], z_peer(k))

    def filt_along_z(k):
        return remote(
            filt_t.at[:, lax.rem(z + k, 8)], filt_z.at[:, SPOT[k]], fz_s.at[k], fz_r.at[k], z_peer(k)
        )

    for k in range(1, 8):
        tok_z(k).start()
    for k in NEAR[1:]:
        filt_along_z(k).start()
    for load in loads[2:]:
        load.wait()
    for half in range(2):
        for part in range(4):
            start = part * 512 + half * 256
            b_half[half, :, :, part * 256 : (part + 1) * 256] = proj_ref[:, :, start : start + 256]
    stacked = [tin_ref[s, :, pl.ds(lanes, 128)] for s in range(3)] + [skip_ref[pl.ds(ctx // 4, 1), :]]
    tin_t[...] = jnp.concatenate(stacked + [jnp.zeros((6, 128), F32)], 0).T
    for s in range(3):
        tout_ref[3 * s : 3 * s + 3, :] = tpr_ref[s]
    tout_ref[9:16, :] = tsh_ref[...]
    tout_ref[16:17, :] = jnp.concatenate([ssk_ref[0:1, :], ssk_ref[1:2, :]], 1)
    tout_ref[17:24, :] = jnp.zeros((7, 256), F32)
    rows = pl.multiple_of((ctx % 4) * 32, 32)
    tin = tin_t[pl.ds(rows, 32), :]

    swap = remote(b_half.at[1 - yl], b_all.at[:, yl, z], sw_s, sw_r, dev(x, 1 - yl, z, ch))
    swap.start()
    taps_copy = remote(tout_ref, taps_mine, tp_s, tp_r, turned)
    pl.when(is_turned)(lambda: taps_copy.start())

    @pl.when(x == ch)
    def _():
        taps_mine[...] = tout_ref[...]

    b_all[:, yl, z] = b_half[yl]
    for other in range(8):
        filt_z[other, 0] = filt_t[other, z]
    tab_copy.wait()
    for j in range(3):
        tab_t[...] = tab_buf[j].T
        spec[pl.ds(32 * j, 32), 0:512] = tab_t[pl.ds(rows, 32), :].astype(F32)
    table = jnp.concatenate([spec[0:96, 0:256], spec[0:96, 256:512]], 0).astype(BF16)

    def tok_x(k):
        line = tok_all.at[pl.ds(xy * 8, 8)]
        return remote(line, line, tx_s.at[k], tx_r.at[k], xy_peer(k))

    for k in range(1, 8):
        tok_z(k).wait()
    for k in range(1, 8):
        tok_x(k).start()

    def filt_over_x(wave, k):
        spots = pl.ds(WAVES[wave], WAVES[wave + 1] - WAVES[wave])
        other = lax.rem(xy + k, 8)
        return remote(
            filt_z.at[other, spots], filt_x.at[xy, spots], fx_s.at[wave, k], fx_r.at[wave, k], xy_peer(k)
        )

    def ring(direction, step):
        which = lax.rem(z + (8 - step if direction > 0 else step), 8)
        chunk = b_all.at[:, :, which] if step < 3 else b_all.at[:, 0 if direction > 0 else 1, which]
        sems = (bp_s if direction > 0 else bm_s).at[step]
        return remote(chunk, chunk, sems, b_r.at[direction, step], z_peer(1 if direction > 0 else 7))

    def ring_on(step):
        for direction in (1, 0):
            ring(direction, step).wait()
            if step < 3:
                ring(direction, step + 1).start()

    swap.wait()
    ring(1, 0).start()
    ring(0, 0).start()

    for k in range(1, 8):
        tok_x(k).wait()

    def embed(chunk, carry):
        ids = jnp.concatenate([tok_all[chunk * 4 + i] for i in range(4)], 1)
        upper = ids >= 256
        hot = (lax.broadcasted_iota(jnp.int32, (256, 512), 0) == jnp.where(upper, ids - 256, ids))
        both = dot(table, hot.astype(F32).astype(BF16))
        value = jnp.where(upper, both[96:], both[:96])
        wide = jnp.concatenate([carry, value], 1)
        total = None
        parts = []
        for j in range(3):
            total = tin[:, j : j + 1] * value[32 * j : 32 * j + 32]
            for s in (1, 2):
                moved = pltpu.roll(wide[32 * j : 32 * j + 32], s, 1)[:, 128:]
                total = total + tin[:, 3 * s + j : 3 * s + j + 1] * moved
            parts.append(total)
        gate = (parts[1] * parts[2]).astype(BF16).astype(F32)
        for i in range(4):
            at = pl.ds(pl.multiple_of((chunk * 4 + i) * 32, 32), 32)
            gated[at, :] = gate[:, i * 128 : (i + 1) * 128]
            query[at, :] = parts[0][:, i * 128 : (i + 1) * 128]
        return value[:, 384:]

    def wave_on(wave):
        for k in NEAR[max(1, WAVES[wave]) : WAVES[wave + 1]]:
            filt_along_z(k).wait()
        for k in range(1, 8):
            filt_over_x(wave, k).start()

    carry = lax.fori_loop(0, 8, embed, jnp.zeros((96, 128), F32))
    wave_on(0)
    carry = lax.fori_loop(8, 12, embed, carry)
    wave_on(1)
    lax.fori_loop(12, 16, embed, carry)
    wave_on(2)
    filt_x[xy] = filt_z[xy]

    def first():
        return dft_ref[0:128, :]

    def last():
        return jnp.concatenate([dft_ref[128:192, :], dft_ref[192:256, :]], 1)

    def inner():
        return jnp.concatenate([dft_ref[256:512, :], dft_ref[512:768, :]], 1)

    def turns():
        return turn_ref[0:64, :], turn_ref[64:128, :]

    def forward(source, group):
        columns = [source[pl.ds(group * 8 + i, 64, stride=32), :] for i in range(8)]
        column = jnp.concatenate(columns, 1).astype(BF16)
        stage = dot(first(), jnp.concatenate([column, column], 0))
        cos, sin = turns()
        turned_rows = []
        for i in range(8):
            re, im = stage[:64, i * 128 : (i + 1) * 128], stage[64:, i * 128 : (i + 1) * 128]
            turned_rows.append(jnp.concatenate([re * cos + im * sin, im * cos - re * sin], 1))
        return dot(jnp.concatenate(turned_rows, 0).astype(BF16), inner())

    def signal_side(group, _):
        spec[pl.ds(pl.multiple_of(group * 512, 512), 512), 0:256] = forward(gated, group)
        return 0

    lax.fori_loop(0, 4, signal_side, 0)
    for k in range(1, 8):
        filt_over_x(0, k).wait()
    ring_on(0)
    for wave in (1, 2):
        for k in range(1, 8):
            filt_over_x(wave, k).wait()
    for other in range(8):
        for spot in range(8):
            from_z = lax.rem(z + 8 - NEAR[spot], 8)
            at = pl.ds(pl.multiple_of((other * 8 + from_z) * 32, 32), 32)
            filt_f[at, :] = filt_x[other, spot].astype(F32)

    def filter_side(group, _):
        h = forward(filt_f, group)
        s = spec[pl.ds(pl.multiple_of(group * 512, 512), 512), 0:256]
        sr, si, hr, hi = s[:, :128], s[:, 128:], h[:, :128], h[:, 128:]
        product = jnp.concatenate([sr * hr - si * hi, sr * hi + si * hr], 1).astype(BF16)
        back = dot_t(product, inner())
        cos, sin = turns()
        parts = []
        for i in range(8):
            re, im = back[i * 64 : (i + 1) * 64, :128], back[i * 64 : (i + 1) * 64, 128:]
            parts.append(jnp.concatenate([re * cos - im * sin, im * cos + re * sin], 0))
        column = jnp.concatenate(parts, 1).astype(BF16)
        result = dot(last(), jnp.concatenate([column, column], 0)) * (1.0 / 8192)
        for i in range(8):
            long_f[pl.ds(group * 8 + i, 64, stride=32), :] = result[:, i * 128 : (i + 1) * 128]
        return 0

    lax.fori_loop(0, 4, filter_side, 0)

    skip = jnp.broadcast_to(tin[:, 9:10], (32, 128))
    for index in range(64):
        x_, yl_, z_ = index // 16, (index // 8) % 2, index % 8
        at = pl.ds(index * 32, 32)
        rounded = long_f[at, :].astype(BF16).astype(F32)
        value = (query[at, :] * (rounded + skip * gated[at, :])).astype(BF16)
        send_a[(x_ // 2) * 2 + yl_, x_ % 2, z_] = value

    order = [lax.rem(y + off, 4) for off in (2, 1, 3, 0)]

    def a_z(t, k):
        q = order[t]
        return remote(
            send_a.at[q, :, lax.rem(z + k, 8)], all_a.at[x, q, :, z], az_s.at[t, k], az_r.at[t, k], z_peer(k)
        )

    def a_x(t, right):
        mine = all_a.at[x, order[t]]
        return remote(mine, mine, ax_s.at[t, right], ax_r.at[t, right], x_peer(1 if right else 3))

    def a_on(t, right):
        half = all_a.at[lax.rem(x + (3 if right else 1), 4), order[t], right]
        return remote(half, half, ax_s.at[t, 2 + right], ax_r.at[t, 2 + right], x_peer(1 if right else 3))

    def pass_on(t):
        for right in (1, 0):
            a_x(t, right).wait()
            a_on(t, right).start()

    def start_a_z(t):
        for k in NEAR[1:]:
            a_z(t, k).start()
        all_a[x, order[t], :, z] = send_a[order[t], :, z]

    def last_block(part):
        return 1 - core if part == 0 else core

    def last_z(part, k):
        return remote(
            send_a.at[order[3], last_block(part), lax.rem(z + k, 8)],
            all_a.at[x, order[3], last_block(part), z],
            lz_s.at[part, k], lz_r.at[part, k], z_peer(k),
        )

    def last_x(part, k):
        mine = all_a.at[x, order[3], last_block(part)]
        return remote(mine, mine, lx_s.at[part, k], lx_r.at[part, k], x_peer(k))

    def start_last_z(part):
        for k in NEAR[1:]:
            last_z(part, k).start()
        all_a[x, order[3], last_block(part), z] = send_a[order[3], last_block(part), z]

    def last_z_to_x(part):
        for k in NEAR[1:]:
            last_z(part, k).wait()
        for k in (1, 3, 2):
            last_x(part, k).start()

    def last_multiply(part):
        for k in (1, 3, 2):
            last_x(part, k).wait()
        block = jnp.concatenate([all_a[xs, order[3], last_block(part)].reshape(256, 128) for xs in range(4)], 0)
        return dot(b_all[...].reshape(768, 1024), block)

    start_a_z(0)
    start_a_z(1)
    ring_on(1)

    def c_core(t):
        return remote(c_send.at[t], c_recv.at[t], cc_s.at[t], cc_r.at[t], core_peer)

    def c_y(t):
        return remote(y_send.at[t], y_recv.at[t], cy_s.at[t], cy_r.at[t], y_peer((2, 1, 3)[t]))

    def after_core(t):
        c_core(t).wait()
        total = c_mine[t] + c_recv[t].astype(F32)
        y_send[t] = total.astype(BF16)
        c_y(t).start()

    def z_to_x(t):
        for k in NEAR[1:]:
            a_z(t, k).wait()
        for right in (1, 0):
            a_x(t, right).start()

    def multiply(t):
        for right in (1, 0):
            a_on(t, right).wait()

        total = None
        for xs in range(4):
            blocks = [all_a[xs, order[t], lo].reshape(256, 128) for lo in range(2)]
            weights = b_all[...].reshape(768, 1024)[:, xs * 256 : (xs + 1) * 256]
            term = dot(weights, jnp.concatenate(blocks, 1))
            total = term if total is None else total + term

        @pl.when(core == 0)
        def _():
            c_mine[t] = total[:, :128]
            c_send[t] = total[:, 128:].astype(BF16)

        @pl.when(core == 1)
        def _():
            c_mine[t] = total[:, 128:]
            c_send[t] = total[:, :128].astype(BF16)

        c_core(t).start()

    z_to_x(0)
    start_a_z(2)
    z_to_x(1)
    pass_on(0)
    ring_on(2)
    start_last_z(0)
    start_last_z(1)
    pass_on(1)
    z_to_x(2)
    ring_on(3)
    multiply(0)
    multiply(1)
    pass_on(2)
    last_z_to_x(0)
    after_core(0)
    last_z_to_x(1)
    after_core(1)
    multiply(2)
    c_send[3] = last_multiply(0).astype(BF16)
    c_core(3).start()
    after_core(2)
    summed = last_multiply(1)
    c_core(3).wait()
    summed += c_recv[3].astype(F32)
    for t in range(3):
        c_y(t).wait()
        summed += y_recv[t].astype(F32)
    projected = jnp.concatenate([summed[i * 128 : (i + 1) * 128].T for i in range(6)], 1).astype(BF16)

    halo = remote(halo_send, halo_recv, h_s, h_r, owner(place + 1))
    halo_send[...] = projected[112:]
    pl.when(has_next)(lambda: halo.start())

    pl.when(is_turned)(lambda: taps_copy.wait())

    def shifted(value, s):
        return value if s == 0 else pltpu.roll(value, s, 0)

    def mix(wide):
        feats = []
        for j in range(3):
            part = wide[:, j * 256 : (j + 1) * 256].astype(F32)
            total = None
            for s in range(3):
                term = taps_mine[3 * s + j : 3 * s + j + 1, :] * shifted(part, s)
                total = term if total is None else total + term
            feats.append(total)
        gate = feats[1] * feats[2]
        short = None
        for s in range(7):
            term = taps_mine[9 + s : 10 + s, :] * shifted(gate, s)
            short = term if short is None else short + term
        return (feats[0] * (short + taps_mine[16:17, :] * gate))[16:].astype(BF16)

    def out_copy(part):
        at = (pl.ds(16, 112), pl.ds(0, 16))[part]
        return remote(out_send.at[at], out_recv.at[at], o_s.at[part], o_r.at[part], turned)

    out_send[16:] = mix(projected)
    pl.when(is_turned)(lambda: out_copy(0).start())

    @pl.when(place == 0)
    def _():
        halo_recv[...] = jnp.zeros_like(halo_recv)

    pl.when(has_next)(lambda: halo.wait_send())
    pl.when(has_prev)(lambda: halo.wait_recv())
    out_send[0:16] = mix(jnp.concatenate([halo_recv[...], projected[:16]], 0))

    @pl.when(is_turned)
    def _():
        out_copy(1).start()
        out_copy(0).wait()
        out_copy(1).wait()

    @pl.when(x == ch)
    def _():
        out_recv[...] = out_send[...]

    out_ref[...] = out_recv[...]


def per_device(token_ids, tables, filter_long, skip_long, taps_in, projection, taps_proj, taps_short, skip_short):
    vmem = pl.BlockSpec(memory_space=pltpu.VMEM)
    hbm = pl.BlockSpec(memory_space=pltpu.HBM)
    tables_dft = [jnp.asarray(t) for t in dft_tables()]
    dma = pltpu.SemaphoreType.DMA
    scratch = [
        pltpu.VMEM((1, 128), jnp.int32),
        pltpu.VMEM((128, 2048), BF16),
        pltpu.VMEM((3, 3, 2048), F32),
        pltpu.VMEM((16, 128), F32),
        pltpu.VMEM((3, 16, 2048), BF16),
        pltpu.VMEM((3, 3, 256), F32),
        pltpu.VMEM((7, 256), F32),
        pltpu.VMEM((2, 128), F32),
        *[pltpu.VMEM(t.shape, t.dtype) for t in tables_dft],
        pltpu.VMEM((24, 256), F32),
        dma((10,)),
        pltpu.VMEM((64, 1, 128), jnp.int32),
        pltpu.VMEM((3, 512, 128), BF16),
        pltpu.VMEM((128, 512), BF16),
        pltpu.VMEM((128, 16), F32),
        pltpu.VMEM((8, 8, 32, 128), BF16),
        pltpu.VMEM((8, 8, 32, 128), BF16),
        pltpu.VMEM((8, 8, 32, 128), BF16),
        pltpu.VMEM((2048, 128), F32),
        pltpu.VMEM((2048, 128), F32),
        pltpu.VMEM((2048, 128), F32),
        pltpu.VMEM((2048, 128), F32),
        pltpu.VMEM((2048, 512), F32),
        pltpu.VMEM((4, 2, 8, 32, 128), BF16),
        pltpu.VMEM((4, 4, 2, 8, 32, 128), BF16),
        pltpu.VMEM((2, 3, 16, 1024), BF16),
        pltpu.VMEM((3, 2, 8, 16, 1024), BF16),
        pltpu.VMEM((4, 768, 128), BF16),
        pltpu.VMEM((4, 768, 128), BF16),
        pltpu.VMEM((4, 768, 128), F32),
        pltpu.VMEM((3, 768, 128), BF16),
        pltpu.VMEM((3, 768, 128), BF16),
        pltpu.VMEM((24, 256), F32),
        pltpu.VMEM((16, 768), BF16),
        pltpu.VMEM((16, 768), BF16),
        pltpu.VMEM((128, 256), BF16),
        pltpu.VMEM((128, 256), BF16),
        dma, dma((8,)), dma((8,)), dma((8,)), dma((8,)),
        dma((8,)), dma((8,)), dma((3, 8)), dma((3, 8)),
        dma, dma, dma((4,)), dma((4,)), dma((2, 4)),
        dma((3, 8)), dma((3, 8)), dma((3, 4)), dma((3, 4)),
        dma((4,)), dma((4,)), dma((3,)), dma((3,)),
        dma, dma, dma, dma, dma((2,)), dma((2,)),
        dma((2, 8)), dma((2, 8)), dma((2, 4)), dma((2, 4)),
    ]
    return pl.pallas_call(
        kernel,
        out_shape=jax.ShapeDtypeStruct((128, 256), BF16),
        in_specs=[hbm] * 11,
        out_specs=vmem,
        scratch_shapes=scratch,
        compiler_params=pltpu.CompilerParams(
            collective_id=0, has_side_effects=True, vmem_limit_bytes=60 * 2**20
        ),
    )(
        token_ids.reshape(1, 128), jnp.transpose(tables, (1, 0, 2)), filter_long, taps_in,
        skip_long.reshape(16, 128), jnp.transpose(projection, (1, 2, 0)), taps_proj, taps_short,
        skip_short.reshape(2, 128), *tables_dft,
    )


def solution(mesh):
    placed = (
        P("ctx"),
        P(None, None, "ch"),
        P("ctx", "ch"),
        P("ch"),
        P(None, None, "ch"),
        P("ch", None, "ctx"),
        P(None, None, "ch"),
        P(None, "ch"),
        P("ch"),
    )
    return jax.shard_map(
        per_device, mesh=mesh, in_specs=placed, out_specs=P("ctx", "ch"), check_vma=False
    )
```

```python
import functools

import jax
import jax.numpy as jnp
import numpy as np
from jax import lax
from jax.experimental import pallas as pl
from jax.experimental.pallas import tpu as pltpu
from jax.sharding import PartitionSpec as P

MESH = pl.DeviceIdType.MESH
F32, BF16 = jnp.float32, jnp.bfloat16
NEAR = (0, 1, 7, 2, 6, 3, 5, 4)
WAVES = (0, 5, 7, 8)
SPOT = tuple(NEAR.index(k) for k in range(8))


def dft_tables():
    k1 = np.arange(64)[:, None] + 0.25
    phase = 2 * np.pi * k1 * np.arange(64)[None, :] / 64
    rows = np.concatenate([np.cos(phase), -np.sin(phase)], 0)

    def split(table):
        high = table.astype(BF16)
        return high, (table - high.astype(np.float64)).astype(BF16)

    high, low = split(rows)
    first = np.concatenate([high, low], 1)
    turn = 2 * np.pi * k1 * np.arange(128)[None, :] / 8192
    inner = 2 * np.pi * np.outer(np.arange(128), np.arange(128)) / 128
    cos, sin = np.cos(inner), np.sin(inner)
    both = np.concatenate([np.concatenate([cos, -sin], 1), np.concatenate([sin, cos], 1)], 0)
    w_high = both.astype(BF16)
    tall = [first, high.T, low.T, *np.split(w_high, 2, 1)]
    return np.concatenate(tall, 0), np.concatenate([np.cos(turn), np.sin(turn)], 0).astype(np.float32)


def dot(left, right):
    return jnp.dot(left, right, preferred_element_type=F32)


def dot_t(left, right):
    return lax.dot_general(left, right, (((1,), (1,)), ((), ())), preferred_element_type=F32)


def kernel(
    tok_hbm, tab_hbm, filt_hbm, tin_hbm, skip_hbm, proj_hbm, tpr_hbm, tsh_hbm, ssk_hbm,
    dft_hbm, turn_hbm,
    out_ref,
    tok_ref, filt_ref, tin_ref, skip_ref, proj_ref, tpr_ref, tsh_ref, ssk_ref,
    dft_ref, turn_ref, tout_ref, load_sem,
    tok_all, tab_buf, tab_t, tin_t, filt_t, filt_z, filt_x, filt_f, gated, query, long_f,
    spec, send_a, all_a, b_half, b_all, c_send, c_recv, c_mine, y_send, y_recv,
    taps_mine, halo_send, halo_recv, out_send, out_recv,
    tab_sem, tz_s, tz_r, tx_s, tx_r, fz_s, fz_r, fx_s, fx_r, sw_s, sw_r, bp_s, bm_s, b_r,
    az_s, az_r, ax_s, ax_r, cc_s, cc_r, cy_s, cy_r, tp_s, tp_r, h_s, h_r, o_s, o_r,
    lz_s, lz_r, lx_s, lx_r,
):
    ctx, ch = lax.axis_index("ctx"), lax.axis_index("ch")
    x, yl, z = ctx // 16, (ctx // 8) % 2, ctx % 8
    yh, core = ch // 2, ch % 2
    xy = x * 2 + yl
    y = yh * 2 + yl

    def dev(x_, yl_, z_, ch_):
        return {"ctx": x_ * 16 + yl_ * 8 + z_, "ch": ch_}

    def z_peer(k):
        return dev(x, yl, lax.rem(z + k, 8), ch)

    def xy_peer(k):
        other = lax.rem(xy + k, 8)
        return dev(other // 2, other % 2, z, ch)

    def x_peer(k):
        return dev(lax.rem(x + k, 4), yl, z, ch)

    core_peer = dev(x, yl, z, yh * 2 + 1 - core)

    def y_peer(k):
        other = lax.rem(y + k, 4)
        return dev(x, other % 2, z, (other // 2) * 2 + core)

    turned = dev(ch, yl, z, x)
    is_turned = x != ch
    place = ch * 16 + yl * 8 + z

    def owner(index):
        return dev(x, (index // 8) % 2, index % 8, index // 16)

    has_next, has_prev = place < 63, place > 0

    def remote(src, dst, send, recv, device):
        return pltpu.make_async_remote_copy(
            src_ref=src, dst_ref=dst, send_sem=send, recv_sem=recv, device_id=device, device_id_type=MESH
        )

    lanes = pl.multiple_of((ctx // 4) * 128, 128)
    tab_copy = pltpu.make_async_copy(tab_hbm.at[:, :, pl.ds(lanes, 128)], tab_buf, tab_sem)
    pairs = (
        (filt_hbm, filt_ref), (tok_hbm, tok_ref), (proj_hbm, proj_ref), (tin_hbm, tin_ref),
        (skip_hbm, skip_ref), (tpr_hbm, tpr_ref), (tsh_hbm, tsh_ref), (ssk_hbm, ssk_ref),
        (dft_hbm, dft_ref), (turn_hbm, turn_ref),
    )
    loads = [pltpu.make_async_copy(src, dst, load_sem.at[i]) for i, (src, dst) in enumerate(pairs)]
    loads[0].start()

    bar = pltpu.get_barrier_semaphore()

    def greet(device):
        pl.semaphore_signal(bar, inc=1, device_id=device, device_id_type=MESH)

    for k in range(1, 8):
        greet(z_peer(k))
        greet(xy_peer(k))
    greet(dev(x, yl, z, (1 - yh) * 2 + core))
    greet(dev(x, 1 - yl, z, (1 - yh) * 2 + core))
    greet(core_peer)
    pl.when(is_turned)(lambda: greet(turned))
    pl.when((z == 7) & has_next)(lambda: greet(owner(place + 1)))
    pl.when((z == 0) & has_prev)(lambda: greet(owner(place - 1)))

    for load in loads[1:]:
        load.start()
    tab_copy.start()
    loads[0].wait()
    for group in range(16):
        block = filt_ref[:, group * 128 : (group + 1) * 128].T
        for part in range(4):
            index = group * 4 + part
            filt_t[index // 8, index % 8] = block[part * 32 : (part + 1) * 32]
    loads[1].wait()
    tok_all[ctx] = tok_ref[...]
    expected = 17 + jnp.where(is_turned, 1, 0)
    expected += jnp.where((z == 7) & has_next, 1, 0) + jnp.where((z == 0) & has_prev, 1, 0)
    pl.semaphore_wait(bar, expected)

    def tok_z(k):
        return remote(tok_all.at[ctx], tok_all.at[ctx], tz_s.at[k], tz_r.at[k], z_peer(k))

    def filt_along_z(k):
        return remote(
            filt_t.at[:, lax.rem(z + k, 8)], filt_z.at[:, SPOT[k]], fz_s.at[k], fz_r.at[k], z_peer(k)
        )

    for k in range(1, 8):
        tok_z(k).start()
    for k in NEAR[1:]:
        filt_along_z(k).start()
    for load in loads[2:]:
        load.wait()
    for half in range(2):
        for part in range(4):
            start = part * 512 + half * 256
            b_half[half, :, :, part * 256 : (part + 1) * 256] = proj_ref[:, :, start : start + 256]
    stacked = [tin_ref[s, :, pl.ds(lanes, 128)] for s in range(3)] + [skip_ref[pl.ds(ctx // 4, 1), :]]
    tin_t[...] = jnp.concatenate(stacked + [jnp.zeros((6, 128), F32)], 0).T
    for s in range(3):
        tout_ref[3 * s : 3 * s + 3, :] = tpr_ref[s]
    tout_ref[9:16, :] = tsh_ref[...]
    tout_ref[16:17, :] = jnp.concatenate([ssk_ref[0:1, :], ssk_ref[1:2, :]], 1)
    tout_ref[17:24, :] = jnp.zeros((7, 256), F32)
    rows = pl.multiple_of((ctx % 4) * 32, 32)
    tin = tin_t[pl.ds(rows, 32), :]

    swap = remote(b_half.at[1 - yl], b_all.at[:, yl, z], sw_s, sw_r, dev(x, 1 - yl, z, ch))
    swap.start()
    taps_copy = remote(tout_ref, taps_mine, tp_s, tp_r, turned)
    pl.when(is_turned)(lambda: taps_copy.start())

    @pl.when(x == ch)
    def _():
        taps_mine[...] = tout_ref[...]

    b_all[:, yl, z] = b_half[yl]
    for other in range(8):
        filt_z[other, 0] = filt_t[other, z]
    tab_copy.wait()
    for j in range(3):
        tab_t[...] = tab_buf[j].T
        spec[pl.ds(32 * j, 32), 0:512] = tab_t[pl.ds(rows, 32), :].astype(F32)
    table = jnp.concatenate([spec[0:96, 0:256], spec[0:96, 256:512]], 0).astype(BF16)

    def tok_x(k):
        line = tok_all.at[pl.ds(xy * 8, 8)]
        return remote(line, line, tx_s.at[k], tx_r.at[k], xy_peer(k))

    for k in range(1, 8):
        tok_z(k).wait()
    for k in range(1, 8):
        tok_x(k).start()

    def filt_over_x(wave, k):
        spots = pl.ds(WAVES[wave], WAVES[wave + 1] - WAVES[wave])
        other = lax.rem(xy + k, 8)
        return remote(
            filt_z.at[other, spots], filt_x.at[xy, spots], fx_s.at[wave, k], fx_r.at[wave, k], xy_peer(k)
        )

    def ring(direction, step):
        which = lax.rem(z + (8 - step if direction > 0 else step), 8)
        chunk = b_all.at[:, :, which] if step < 3 else b_all.at[:, 0 if direction > 0 else 1, which]
        sems = (bp_s if direction > 0 else bm_s).at[step]
        return remote(chunk, chunk, sems, b_r.at[direction, step], z_peer(1 if direction > 0 else 7))

    def ring_on(step):
        for direction in (1, 0):
            ring(direction, step).wait()
            if step < 3:
                ring(direction, step + 1).start()

    swap.wait()
    ring(1, 0).start()
    ring(0, 0).start()

    for k in range(1, 8):
        tok_x(k).wait()

    def embed(chunk, carry):
        ids = jnp.concatenate([tok_all[chunk * 4 + i] for i in range(4)], 1)
        upper = ids >= 256
        hot = (lax.broadcasted_iota(jnp.int32, (256, 512), 0) == jnp.where(upper, ids - 256, ids))
        both = dot(table, hot.astype(F32).astype(BF16))
        value = jnp.where(upper, both[96:], both[:96])
        wide = jnp.concatenate([carry, value], 1)
        total = None
        parts = []
        for j in range(3):
            total = tin[:, j : j + 1] * value[32 * j : 32 * j + 32]
            for s in (1, 2):
                moved = pltpu.roll(wide[32 * j : 32 * j + 32], s, 1)[:, 128:]
                total = total + tin[:, 3 * s + j : 3 * s + j + 1] * moved
            parts.append(total)
        gate = (parts[1] * parts[2]).astype(BF16).astype(F32)
        for i in range(4):
            at = pl.ds(pl.multiple_of((chunk * 4 + i) * 32, 32), 32)
            gated[at, :] = gate[:, i * 128 : (i + 1) * 128]
            query[at, :] = parts[0][:, i * 128 : (i + 1) * 128]
        return value[:, 384:]

    def wave_on(wave):
        for k in NEAR[max(1, WAVES[wave]) : WAVES[wave + 1]]:
            filt_along_z(k).wait()
        for k in range(1, 8):
            filt_over_x(wave, k).start()

    carry = lax.fori_loop(0, 8, embed, jnp.zeros((96, 128), F32))
    wave_on(0)
    carry = lax.fori_loop(8, 12, embed, carry)
    wave_on(1)
    lax.fori_loop(12, 16, embed, carry)
    wave_on(2)
    filt_x[xy] = filt_z[xy]

    def first():
        return dft_ref[0:128, :]

    def last():
        return jnp.concatenate([dft_ref[128:192, :], dft_ref[192:256, :]], 1)

    def inner():
        return jnp.concatenate([dft_ref[256:512, :], dft_ref[512:768, :]], 1)

    def turns():
        return turn_ref[0:64, :], turn_ref[64:128, :]

    def forward(source, group):
        columns = [source[pl.ds(group * 8 + i, 64, stride=32), :] for i in range(8)]
        column = jnp.concatenate(columns, 1).astype(BF16)
        stage = dot(first(), jnp.concatenate([column, column], 0))
        cos, sin = turns()
        turned_rows = []
        for i in range(8):
            re, im = stage[:64, i * 128 : (i + 1) * 128], stage[64:, i * 128 : (i + 1) * 128]
            turned_rows.append(jnp.concatenate([re * cos + im * sin, im * cos - re * sin], 1))
        return dot(jnp.concatenate(turned_rows, 0).astype(BF16), inner())

    def signal_side(group, _):
        spec[pl.ds(pl.multiple_of(group * 512, 512), 512), 0:256] = forward(gated, group)
        return 0

    lax.fori_loop(0, 4, signal_side, 0)
    for k in range(1, 8):
        filt_over_x(0, k).wait()
    ring_on(0)
    for wave in (1, 2):
        for k in range(1, 8):
            filt_over_x(wave, k).wait()
    for other in range(8):
        for spot in range(8):
            from_z = lax.rem(z + 8 - NEAR[spot], 8)
            at = pl.ds(pl.multiple_of((other * 8 + from_z) * 32, 32), 32)
            filt_f[at, :] = filt_x[other, spot].astype(F32)

    def filter_side(group, _):
        h = forward(filt_f, group)
        s = spec[pl.ds(pl.multiple_of(group * 512, 512), 512), 0:256]
        sr, si, hr, hi = s[:, :128], s[:, 128:], h[:, :128], h[:, 128:]
        product = jnp.concatenate([sr * hr - si * hi, sr * hi + si * hr], 1).astype(BF16)
        back = dot_t(product, inner())
        cos, sin = turns()
        parts = []
        for i in range(8):
            re, im = back[i * 64 : (i + 1) * 64, :128], back[i * 64 : (i + 1) * 64, 128:]
            parts.append(jnp.concatenate([re * cos - im * sin, im * cos + re * sin], 0))
        column = jnp.concatenate(parts, 1).astype(BF16)
        result = dot(last(), jnp.concatenate([column, column], 0)) * (1.0 / 8192)
        for i in range(8):
            long_f[pl.ds(group * 8 + i, 64, stride=32), :] = result[:, i * 128 : (i + 1) * 128]
        return 0

    lax.fori_loop(0, 4, filter_side, 0)

    skip = jnp.broadcast_to(tin[:, 9:10], (32, 128))
    for index in range(64):
        x_, yl_, z_ = index // 16, (index // 8) % 2, index % 8
        at = pl.ds(index * 32, 32)
        rounded = long_f[at, :].astype(BF16).astype(F32)
        value = (query[at, :] * (rounded + skip * gated[at, :])).astype(BF16)
        send_a[(x_ // 2) * 2 + yl_, x_ % 2, z_] = value

    order = [lax.rem(y + off, 4) for off in (2, 1, 3, 0)]

    def a_z(t, k):
        q = order[t]
        return remote(
            send_a.at[q, :, lax.rem(z + k, 8)], all_a.at[x, q, :, z], az_s.at[t, k], az_r.at[t, k], z_peer(k)
        )

    def a_x(t, right):
        mine = all_a.at[x, order[t]]
        return remote(mine, mine, ax_s.at[t, right], ax_r.at[t, right], x_peer(1 if right else 3))

    def a_on(t, right):
        half = all_a.at[lax.rem(x + (3 if right else 1), 4), order[t], right]
        return remote(half, half, ax_s.at[t, 2 + right], ax_r.at[t, 2 + right], x_peer(1 if right else 3))

    def pass_on(t):
        for right in (1, 0):
            a_x(t, right).wait()
            a_on(t, right).start()

    def start_a_z(t):
        for k in NEAR[1:]:
            a_z(t, k).start()
        all_a[x, order[t], :, z] = send_a[order[t], :, z]

    def last_block(part):
        return 1 - core if part == 0 else core

    def last_z(part, k):
        return remote(
            send_a.at[order[3], last_block(part), lax.rem(z + k, 8)],
            all_a.at[x, order[3], last_block(part), z],
            lz_s.at[part, k], lz_r.at[part, k], z_peer(k),
        )

    def last_x(part, k):
        mine = all_a.at[x, order[3], last_block(part)]
        return remote(mine, mine, lx_s.at[part, k], lx_r.at[part, k], x_peer(k))

    def start_last_z(part):
        for k in NEAR[1:]:
            last_z(part, k).start()
        all_a[x, order[3], last_block(part), z] = send_a[order[3], last_block(part), z]

    def last_z_to_x(part):
        for k in NEAR[1:]:
            last_z(part, k).wait()
        for k in (1, 3, 2):
            last_x(part, k).start()

    def last_multiply(part):
        for k in (1, 3, 2):
            last_x(part, k).wait()
        block = jnp.concatenate([all_a[xs, order[3], last_block(part)].reshape(256, 128) for xs in range(4)], 0)
        return dot(b_all[...].reshape(768, 1024), block)

    start_a_z(0)
    start_a_z(1)
    ring_on(1)

    def c_core(t):
        return remote(c_send.at[t], c_recv.at[t], cc_s.at[t], cc_r.at[t], core_peer)

    def c_y(t):
        return remote(y_send.at[t], y_recv.at[t], cy_s.at[t], cy_r.at[t], y_peer((2, 1, 3)[t]))

    def after_core(t):
        c_core(t).wait()
        total = c_mine[t] + c_recv[t].astype(F32)
        y_send[t] = total.astype(BF16)
        c_y(t).start()

    def z_to_x(t):
        for k in NEAR[1:]:
            a_z(t, k).wait()
        for right in (1, 0):
            a_x(t, right).start()

    def multiply(t):
        for right in (1, 0):
            a_on(t, right).wait()

        total = None
        for xs in range(4):
            blocks = [all_a[xs, order[t], lo].reshape(256, 128) for lo in range(2)]
            weights = b_all[...].reshape(768, 1024)[:, xs * 256 : (xs + 1) * 256]
            term = dot(weights, jnp.concatenate(blocks, 1))
            total = term if total is None else total + term

        @pl.when(core == 0)
        def _():
            c_mine[t] = total[:, :128]
            c_send[t] = total[:, 128:].astype(BF16)

        @pl.when(core == 1)
        def _():
            c_mine[t] = total[:, 128:]
            c_send[t] = total[:, :128].astype(BF16)

        c_core(t).start()

    z_to_x(0)
    start_a_z(2)
    z_to_x(1)
    pass_on(0)
    ring_on(2)
    start_last_z(0)
    start_last_z(1)
    pass_on(1)
    z_to_x(2)
    ring_on(3)
    multiply(0)
    multiply(1)
    pass_on(2)
    last_z_to_x(0)
    after_core(0)
    last_z_to_x(1)
    after_core(1)
    multiply(2)
    c_send[3] = last_multiply(0).astype(BF16)
    c_core(3).start()
    after_core(2)
    summed = last_multiply(1)
    c_core(3).wait()
    summed += c_recv[3].astype(F32)
    for t in range(3):
        c_y(t).wait()
        summed += y_recv[t].astype(F32)
    projected = jnp.concatenate([summed[i * 128 : (i + 1) * 128].T for i in range(6)], 1).astype(BF16)

    halo = remote(halo_send, halo_recv, h_s, h_r, owner(place + 1))
    halo_send[...] = projected[112:]
    pl.when(has_next)(lambda: halo.start())

    pl.when(is_turned)(lambda: taps_copy.wait())

    def shifted(value, s):
        return value if s == 0 else pltpu.roll(value, s, 0)

    def mix(wide):
        feats = []
        for j in range(3):
            part = wide[:, j * 256 : (j + 1) * 256].astype(F32)
            total = None
            for s in range(3):
                term = taps_mine[3 * s + j : 3 * s + j + 1, :] * shifted(part, s)
                total = term if total is None else total + term
            feats.append(total)
        gate = feats[1] * feats[2]
        short = None
        for s in range(7):
            term = taps_mine[9 + s : 10 + s, :] * shifted(gate, s)
            short = term if short is None else short + term
        return (feats[0] * (short + taps_mine[16:17, :] * gate))[16:].astype(BF16)

    def out_copy(part):
        at = (pl.ds(16, 112), pl.ds(0, 16))[part]
        return remote(out_send.at[at], out_recv.at[at], o_s.at[part], o_r.at[part], turned)

    out_send[16:] = mix(projected)
    pl.when(is_turned)(lambda: out_copy(0).start())

    @pl.when(place == 0)
    def _():
        halo_recv[...] = jnp.zeros_like(halo_recv)

    pl.when(has_next)(lambda: halo.wait_send())
    pl.when(has_prev)(lambda: halo.wait_recv())
    out_send[0:16] = mix(jnp.concatenate([halo_recv[...], projected[:16]], 0))

    @pl.when(is_turned)
    def _():
        out_copy(1).start()
        out_copy(0).wait()
        out_copy(1).wait()

    @pl.when(x == ch)
    def _():
        out_recv[...] = out_send[...]

    out_ref[...] = out_recv[...]


def per_device(token_ids, tables, filter_long, skip_long, taps_in, projection, taps_proj, taps_short, skip_short):
    vmem = pl.BlockSpec(memory_space=pltpu.VMEM)
    hbm = pl.BlockSpec(memory_space=pltpu.HBM)
    tables_dft = [jnp.asarray(t) for t in dft_tables()]
    dma = pltpu.SemaphoreType.DMA
    scratch = [
        pltpu.VMEM((1, 128), jnp.int32),
        pltpu.VMEM((128, 2048), BF16),
        pltpu.VMEM((3, 3, 2048), F32),
        pltpu.VMEM((16, 128), F32),
        pltpu.VMEM((3, 16, 2048), BF16),
        pltpu.VMEM((3, 3, 256), F32),
        pltpu.VMEM((7, 256), F32),
        pltpu.VMEM((2, 128), F32),
        *[pltpu.VMEM(t.shape, t.dtype) for t in tables_dft],
        pltpu.VMEM((24, 256), F32),
        dma((10,)),
        pltpu.VMEM((64, 1, 128), jnp.int32),
        pltpu.VMEM((3, 512, 128), BF16),
        pltpu.VMEM((128, 512), BF16),
        pltpu.VMEM((128, 16), F32),
        pltpu.VMEM((8, 8, 32, 128), BF16),
        pltpu.VMEM((8, 8, 32, 128), BF16),
        pltpu.VMEM((8, 8, 32, 128), BF16),
        pltpu.VMEM((2080, 128), F32),
        pltpu.VMEM((2080, 128), F32),
        pltpu.VMEM((2080, 128), F32),
        pltpu.VMEM((2080, 128), F32),
        pltpu.VMEM((2048, 512), F32),
        pltpu.VMEM((4, 2, 8, 32, 128), BF16),
        pltpu.VMEM((4, 4, 2, 8, 32, 128), BF16),
        pltpu.VMEM((2, 3, 16, 1024), BF16),
        pltpu.VMEM((3, 2, 8, 16, 1024), BF16),
        pltpu.VMEM((4, 768, 128), BF16),
        pltpu.VMEM((4, 768, 128), BF16),
        pltpu.VMEM((4, 768, 128), F32),
        pltpu.VMEM((3, 768, 128), BF16),
        pltpu.VMEM((3, 768, 128), BF16),
        pltpu.VMEM((24, 256), F32),
        pltpu.VMEM((16, 768), BF16),
        pltpu.VMEM((16, 768), BF16),
        pltpu.VMEM((128, 256), BF16),
        pltpu.VMEM((128, 256), BF16),
        dma, dma((8,)), dma((8,)), dma((8,)), dma((8,)),
        dma((8,)), dma((8,)), dma((3, 8)), dma((3, 8)),
        dma, dma, dma((4,)), dma((4,)), dma((2, 4)),
        dma((3, 8)), dma((3, 8)), dma((3, 4)), dma((3, 4)),
        dma((4,)), dma((4,)), dma((3,)), dma((3,)),
        dma, dma, dma, dma, dma((2,)), dma((2,)),
        dma((2, 8)), dma((2, 8)), dma((2, 4)), dma((2, 4)),
    ]
    return pl.pallas_call(
        kernel,
        out_shape=jax.ShapeDtypeStruct((128, 256), BF16),
        in_specs=[hbm] * 11,
        out_specs=vmem,
        scratch_shapes=scratch,
        compiler_params=pltpu.CompilerParams(
            collective_id=0, has_side_effects=True, vmem_limit_bytes=60 * 2**20
        ),
    )(
        token_ids.reshape(1, 128), jnp.transpose(tables, (1, 0, 2)), filter_long, taps_in,
        skip_long.reshape(16, 128), jnp.transpose(projection, (1, 2, 0)), taps_proj, taps_short,
        skip_short.reshape(2, 128), *tables_dft,
    )


def solution(mesh):
    placed = (
        P("ctx"),
        P(None, None, "ch"),
        P("ctx", "ch"),
        P("ch"),
        P(None, None, "ch"),
        P("ch", None, "ctx"),
        P(None, None, "ch"),
        P(None, "ch"),
        P("ch"),
    )
    return jax.shard_map(
        per_device, mesh=mesh, in_specs=placed, out_specs=P("ctx", "ch"), check_vma=False
    )
```
